256 devices in a mesh: pipe: 8 (over z), tile: 32 (over x, y, core).
Axes of the slice: x: 4, y: 4, z: 8, core: 2. Of those that a mesh axis runs over, the one named last changes fastest.
Arguments:
- x_next: bfloat16 [8, 4096, 8192], P('pipe', 'tile'), may hold values from -6 to 6
- x_saved: bfloat16 [8, 4096, 8192], P('pipe', 'tile'), may hold values from -6 to 6
- pending: bfloat16 [8, 4096, 8192], P('pipe', 'tile'), may hold values from -6 to 6
- gu_rows: int32 [8, 32, 1], P('pipe'), may hold values from 0 to 63, as said below
- gu_cols: int32 [8, 32, 1], P('pipe'), may hold values from 0 to 111
- gu_live: int32 [8, 32], P('pipe'), may hold values from 1 to 1, as said below
- down_rows: int32 [8, 32, 1], P('pipe'), may hold values from 0 to 111, as said below
- down_cols: int32 [8, 32, 1], P('pipe'), may hold values from 0 to 63
- down_live: int32 [8, 32], P('pipe'), may hold values from 1 to 1, as said below
- gate_up_tiles: bfloat16 [8, 32, 1, 2, 128, 128], P('pipe', 'tile'), may hold values from -0.5 to 0.5
- down_tiles: bfloat16 [8, 32, 1, 128, 128], P('pipe', 'tile'), may hold values from -0.5 to 0.5
Outputs:
- y_next: bfloat16 [8, 4096, 8192], P('pipe', 'tile')
- dx_saved: bfloat16 [8, 4096, 8192], P('pipe', 'tile')
- grad_gate_up: float32 [8, 32, 1, 2, 128, 128], P('pipe', 'tile')
- grad_down: float32 [8, 32, 1, 128, 128], P('pipe', 'tile')
The draws below stay inside these ranges and needn't reach their ends.
Inputs may be any that keep to these rules, and one draw needn't show every extreme that they name: Within a section the 32 x 1 slots of the gate and up lists name distinct tiles (gu_rows, gu_cols). Within a section the 32 x 1 slots of the down list name distinct tiles (down_rows, down_cols). `gu_live`: in every section some owner has all 1 slots live. `down_live`: in every section some owner has all 1 slots live.
All inputs are finite; a program needn't handle non-finite values.
Results may differ from the reference program's by a relative error of at most 0.0067.
Values may be sent and summed in bfloat16 or wider, within the bound.
No kernel may reach another device: no remote copies, remote signals or barrier semaphores. Data moves between devices by JAX's collectives and lax.ppermute only.
A program may use at most 128 MiB of HBM per device.

```python
import jax
import jax.numpy as jnp

D = 8192
FF = 14336
BLOCK = 128
TILE_DEV = 1
SECTIONS = 8
OWNERS = 32
TOKENS = 4096


def tile_positions(key, salt, rows, cols):
    keys = jax.random.split(jax.random.fold_in(key, salt), SECTIONS)

    def one_section(section_key):
        return jax.random.permutation(section_key, rows * cols)[:OWNERS * TILE_DEV]
    positions = jax.vmap(one_section)(keys)
    return positions.reshape(SECTIONS, OWNERS, TILE_DEV).astype(jnp.int32)


def live_counts(key, salt):
    first_key, second_key = jax.random.split(jax.random.fold_in(key, salt))
    lowest = max(1, TILE_DEV // 4)
    counts = jax.random.randint(first_key, (SECTIONS, OWNERS), lowest, TILE_DEV + 1)
    fullest = jax.random.randint(second_key, (SECTIONS,), 0, OWNERS)
    owner_ids = jnp.arange(OWNERS, dtype=jnp.int32)
    return jnp.where(owner_ids[None, :] == fullest[:, None], TILE_DEV, counts).astype(jnp.int32)


def draw_gu_rows(key, part):
    return tile_positions(key, 11, D // BLOCK, FF // BLOCK) // (FF // BLOCK)


def draw_gu_cols(key, part):
    return tile_positions(key, 11, D // BLOCK, FF // BLOCK) % (FF // BLOCK)


def draw_down_rows(key, part):
    return tile_positions(key, 12, FF // BLOCK, D // BLOCK) // (D // BLOCK)


def draw_down_cols(key, part):
    return tile_positions(key, 12, FF // BLOCK, D // BLOCK) % (D // BLOCK)


def draw_gu_live(key, part):
    return live_counts(key, 21)


def draw_down_live(key, part):
    return live_counts(key, 22)


def block_scale(stream_key, extent, cuts, low, top_value):
    factor_of, own = 1.0, jax.random.fold_in(stream_key, 6)
    for axis_at, shards_of in cuts:
        heights = jnp.exp(jax.random.uniform(jax.random.fold_in(own, axis_at), (shards_of,), jnp.float32, low / len(cuts), top_value / len(cuts)))
        factor_of = factor_of * jnp.repeat(heights, extent[axis_at] // shards_of).reshape([-1 if axis == axis_at else 1 for axis in range(len(extent))])
    return factor_of


def bell_draw(rng, extent, deviation, most, cuts=(), kind=jnp.bfloat16):
    factor_of = block_scale(rng, extent, cuts, -0.22, 0.18) if cuts else 1.0
    result = jax.random.normal(rng, extent, jnp.float32) * deviation * factor_of
    return jnp.minimum(jnp.maximum(result, -most), most).astype(kind)


def setup_inputs(seed: int = 0) -> dict:
    streams_of = jax.random.split(jax.random.key(seed), 12)
    return {
        "x_next": bell_draw(streams_of[0], (SECTIONS, TOKENS, D), 1.0, 6.0, ((0, 8), (1, 32))),
        "x_saved": bell_draw(streams_of[1], (SECTIONS, TOKENS, D), 1.0, 6.0, ((0, 8), (1, 32))),
        "pending": bell_draw(streams_of[2], (SECTIONS, TOKENS, D), 1.0, 6.0, ((0, 8), (1, 32))),
        "gu_rows": draw_gu_rows(jax.random.fold_in(streams_of[11], 71), 0),
        "gu_cols": draw_gu_cols(jax.random.fold_in(streams_of[11], 71), 0),
        "gu_live": draw_gu_live(jax.random.fold_in(streams_of[11], 71), 0),
        "down_rows": draw_down_rows(jax.random.fold_in(streams_of[11], 71), 0),
        "down_cols": draw_down_cols(jax.random.fold_in(streams_of[11], 71), 0),
        "down_live": draw_down_live(jax.random.fold_in(streams_of[11], 71), 0),
        "gate_up_tiles": bell_draw(streams_of[9], (SECTIONS, OWNERS, TILE_DEV, 2, BLOCK, BLOCK), (max(BLOCK, BLOCK * OWNERS * TILE_DEV // (FF // BLOCK))) ** -0.5, 0.5, ((0, 8), (1, 32))),
        "down_tiles": bell_draw(streams_of[10], (SECTIONS, OWNERS, TILE_DEV, BLOCK, BLOCK), (max(BLOCK, BLOCK * OWNERS * TILE_DEV // (D // BLOCK))) ** -0.5, 0.5, ((0, 8), (1, 32))),
    }


def column_sum(parts, index, blocks):
    onehot = (index[:, None] == jnp.arange(blocks, dtype=jnp.int32)[None, :]).astype(jnp.float32)
    summed = jnp.einsum('tkq,kc->tcq', parts.astype(jnp.float32), onehot)
    return summed.reshape(parts.shape[0], blocks * parts.shape[2])


def one_section(x_next, x_saved, cot, gu_rows, gu_cols, gu_live, down_rows, down_cols, down_live, gate_up, down):
    count = OWNERS * TILE_DEV
    row_blocks = D // BLOCK
    col_blocks = FF // BLOCK
    g_rows = gu_rows.reshape(count)
    g_cols = gu_cols.reshape(count)
    d_rows = down_rows.reshape(count)
    d_cols = down_cols.reshape(count)
    slot_ids = jnp.arange(TILE_DEV, dtype=jnp.int32)
    g_live = (slot_ids[None, :] < gu_live[:, None]).reshape(count).astype(jnp.float32)
    d_live = (slot_ids[None, :] < down_live[:, None]).reshape(count).astype(jnp.float32)
    weights_gu = gate_up.reshape(count, 2, BLOCK, BLOCK).astype(jnp.float32)
    weights_down = down.reshape(count, BLOCK, BLOCK).astype(jnp.float32)

    def project(inputs):
        x_slots = inputs.reshape(TOKENS, row_blocks, BLOCK)[:, g_rows, :].astype(jnp.float32)
        parts = jnp.einsum('tkp,kgpq->gtkq', x_slots, weights_gu) * g_live[None, None, :, None]
        parts = parts.astype(jnp.bfloat16)
        return column_sum(parts[0], g_cols, col_blocks), column_sum(parts[1], g_cols, col_blocks), x_slots

    gate_next, up_next, unused = project(x_next)
    gate_saved, up_saved, x_slots = project(x_saved)
    sig_next = jax.nn.sigmoid(gate_next)
    hidden_next = (gate_next * sig_next * up_next).astype(jnp.bfloat16)
    sig = jax.nn.sigmoid(gate_saved)
    act = gate_saved * sig
    hidden_saved = (act * up_saved).astype(jnp.bfloat16)

    h_slots = hidden_next.reshape(TOKENS, col_blocks, BLOCK)[:, d_rows, :].astype(jnp.float32)
    y_part = (jnp.einsum('tkp,kpq->tkq', h_slots, weights_down) * d_live[None, :, None]).astype(jnp.bfloat16)
    y_next = column_sum(y_part, d_cols, row_blocks).astype(jnp.bfloat16)

    dy_slots = cot.reshape(TOKENS, row_blocks, BLOCK)[:, d_cols, :].astype(jnp.float32)
    hs_saved = hidden_saved.reshape(TOKENS, col_blocks, BLOCK)[:, d_rows, :].astype(jnp.float32)
    grad_down = jnp.einsum('tkp,tkq->kpq', hs_saved, dy_slots) * d_live[:, None, None]
    dh_part = (jnp.einsum('tkq,kpq->tkp', dy_slots, weights_down) * d_live[None, :, None]).astype(jnp.bfloat16)
    dh = column_sum(dh_part, d_rows, col_blocks)

    d_gate = (dh * up_saved * sig * (1.0 + gate_saved * (1.0 - sig))).astype(jnp.bfloat16)
    d_up = (dh * act).astype(jnp.bfloat16)
    grads = jnp.stack([d_gate, d_up]).reshape(2, TOKENS, col_blocks, BLOCK)[:, :, g_cols, :].astype(jnp.float32)
    grad_gu = jnp.einsum('tkp,gtkq->kgpq', x_slots, grads) * g_live[:, None, None, None]
    dx_part = (jnp.einsum('gtkq,kgpq->tkp', grads, weights_gu) * g_live[None, :, None]).astype(jnp.bfloat16)
    dx_saved = column_sum(dx_part, g_rows, row_blocks).astype(jnp.bfloat16)
    return (y_next, dx_saved, grad_gu.reshape(OWNERS, TILE_DEV, 2, BLOCK, BLOCK),
            grad_down.reshape(OWNERS, TILE_DEV, BLOCK, BLOCK))


def reference(x_next, x_saved, pending, gu_rows, gu_cols, gu_live, down_rows, down_cols, down_live, gate_up_tiles, down_tiles):
    results = []
    for section in range(SECTIONS):
        cot = pending[(section + 1) % SECTIONS]
        results.append(one_section(x_next[section], x_saved[section], cot, gu_rows[section], gu_cols[section], gu_live[section],
                                 down_rows[section], down_cols[section], down_live[section],
                                 gate_up_tiles[section], down_tiles[section]))
    return (jnp.stack([item[0] for item in results]), jnp.stack([item[1] for item in results]),
            jnp.stack([item[2] for item in results]), jnp.stack([item[3] for item in results]))
```

```python
import functools

import jax
import jax.numpy as jnp
from jax import lax
from jax.experimental import pallas as pl
from jax.experimental.pallas import tpu as pltpu
from jax.sharding import PartitionSpec as P

B = 128
F32 = jnp.float32
BF16 = jnp.bfloat16
ROWS, LEAD, FIRST, HSLOT, DCOLS = range(5)


def loop(count, unroll, body):
    def group(i, carry):
        body([i * unroll + u for u in range(unroll)])
        return carry

    lax.fori_loop(0, count // unroll, group, 0)


def cols(block_index):
    return pl.ds(pl.multiple_of(block_index * B, B), B)


def rounded(value):
    return value.astype(BF16).astype(F32)


def dot(a, b, contract_a, contract_b):
    return lax.dot_general(
        a, b, (((contract_a,), (contract_b,)), ((), ())), preferred_element_type=F32
    )


def vmem(value):
    return pltpu.with_memory_space_constraint(value, pltpu.VMEM)


def call(body, outs, scratch, args, limit, flops=0):
    specs = [pl.BlockSpec(memory_space=pltpu.SMEM)] + [
        pl.BlockSpec(memory_space=pltpu.VMEM) for _ in args[1:]
    ]
    out = pl.pallas_call(
        body,
        out_shape=[o for o, _ in outs],
        in_specs=specs,
        out_specs=[pl.BlockSpec(memory_space=pltpu.VMEM) for _ in outs],
        scratch_shapes=scratch,
        compiler_params=pltpu.CompilerParams(vmem_limit_bytes=limit << 20),
        cost_estimate=pl.CostEstimate(flops=flops, bytes_accessed=1 << 20, transcendentals=0),
    )(args[0], *[vmem(a) for a in args[1:]])
    return out


def out_vmem(shape, dtype):
    return (pltpu.VMEM(shape, dtype), True)


def out_hbm(shape, dtype):
    return (jax.ShapeDtypeStruct(shape, dtype), False)


def pick_kernel(n, tab, pending, out):
    for k in range(n):
        out[k] = pending[0, :, cols(tab[DCOLS, k])]


def forward_kernel(n, tab, x_next, x_saved, w, coef, h_saved, y, acc, h_next, y_acc):
    def project(ks):
        parts = []
        for k in ks:
            at = cols(tab[ROWS, k])
            x = jnp.concatenate([x_next[0, :, at], x_saved[0, :, at]], axis=0)
            parts.append(rounded(dot(x, w[k, :, : 2 * B], 1, 0)))
        for k, part in zip(ks, parts):
            lead = tab[LEAD, k]
            acc[lead] = jnp.where(tab[FIRST, k] == 1, part, acc[lead] + part)

    loop(n, 4, project)

    def activate(ks):
        for k in ks:

            @pl.when(tab[FIRST, k] == 1)
            def _():
                gate, up = acc[k, :B, :B], acc[k, :B, B:]
                h_next[k] = (gate * jax.nn.sigmoid(gate) * up).astype(BF16)
                gate, up = acc[k, B:, :B], acc[k, B:, B:]
                sig = jax.nn.sigmoid(gate)
                act = gate * sig
                h_saved[k] = (act * up).astype(BF16)
                coef[k, :, :B] = up * sig * (1.0 + gate * (1.0 - sig))
                coef[k, :, B:] = act

    loop(n, 1, activate)
    h_next[n] = jnp.zeros((B, B), BF16)
    h_saved[n] = jnp.zeros((B, B), BF16)
    y_acc[...] = jnp.zeros_like(y_acc)

    def down(js):
        parts = [rounded(dot(h_next[tab[HSLOT, j]], w[j, :, 2 * B :], 1, 0)) for j in js]
        for j, part in zip(js, parts):
            y_acc[tab[DCOLS, j]] += part

    loop(n, 4, down)
    for c in range(y_acc.shape[0]):
        y[0, :, c * B : (c + 1) * B] = y_acc[c].astype(BF16)


def backward_kernel(n, tab, x_saved, w, coef, h_saved, cot, parts_out, d_gu, dh):
    dh[...] = jnp.zeros_like(dh)

    def down(js):
        parts = []
        for j in js:
            c = cot[j]
            parts.append(rounded(dot(c, w[j, :, 2 * B :], 1, 1)))
            parts_out[j, :, 2 * B :] = dot(h_saved[tab[HSLOT, j]], c, 0, 0).astype(BF16)
        for j, part in zip(js, parts):
            dh[tab[HSLOT, j]] += part

    loop(n, 4, down)

    def scale(ks):
        for k in ks:

            @pl.when(tab[FIRST, k] == 1)
            def _():
                d_gu[k, :, :B] = (dh[k] * coef[k, :, :B]).astype(BF16)
                d_gu[k, :, B:] = (dh[k] * coef[k, :, B:]).astype(BF16)

    loop(n, 1, scale)

    def grads(ks):
        for k in ks:
            x = x_saved[0, :, cols(tab[ROWS, k])]
            parts_out[k, :, : 2 * B] = dot(x, d_gu[tab[LEAD, k]], 0, 0).astype(BF16)

    loop(n, 4, grads)


def dx_kernel(n, tab, d_gu, w, dx, acc):
    acc[...] = jnp.zeros_like(acc)

    def back(ks):
        parts = [rounded(dot(d_gu[tab[LEAD, k]], w[k, :, : 2 * B], 1, 1)) for k in ks]
        for k, part in zip(ks, parts):
            acc[tab[ROWS, k]] += part

    loop(n, 4, back)
    for c in range(acc.shape[0]):
        dx[0, :, c * B : (c + 1) * B] = acc[c].astype(BF16)


def total_kernel(n, tab, got, grad_gu, grad_down):
    total = got[0].astype(F32)
    for k in range(1, n):
        total += got[k].astype(F32)
    g_live = tab[0, 0].astype(F32)
    d_live = tab[0, 1].astype(F32)
    grad_gu[0, 0, 0, 0] = total[:, :B] * g_live
    grad_gu[0, 0, 0, 1] = total[:, B : 2 * B] * g_live
    grad_down[0, 0, 0] = total[:, 2 * B :] * d_live


def tables(g_rows, g_cols, d_rows, d_cols):
    n = g_rows.shape[0]
    ids = jnp.arange(n, dtype=jnp.int32)
    lead = jnp.min(jnp.where(g_cols[:, None] == g_cols[None, :], ids[None, :], n), axis=1)
    first = (lead == ids).astype(jnp.int32)
    hslot = jnp.min(jnp.where(d_rows[:, None] == g_cols[None, :], ids[None, :], n), axis=1)
    return jnp.stack([g_rows, lead, first, hslot, d_cols])


def per_device(
    x_next,
    x_saved,
    pending,
    gu_rows,
    gu_cols,
    gu_live,
    down_rows,
    down_cols,
    down_live,
    gate_up_tiles,
    down_tiles,
):
    n = lax.axis_size("tile")
    sections = lax.axis_size("pipe")
    mine = lax.axis_index("tile")
    width = x_next.shape[2]
    blocks = width // B
    tok = x_next.shape[1]
    partial = functools.partial

    g_live = (lax.dynamic_index_in_dim(gu_live[0], mine, 0, keepdims=False) > 0).astype(jnp.int32)
    d_live = (lax.dynamic_index_in_dim(down_live[0], mine, 0, keepdims=False) > 0).astype(jnp.int32)
    live = jnp.stack([g_live, d_live])[None, :]
    tab = tables(
        gu_rows[0].reshape(-1), gu_cols[0].reshape(-1), down_rows[0].reshape(-1), down_cols[0].reshape(-1)
    )

    own = jnp.concatenate(
        [
            gate_up_tiles[0, 0, 0, 0] * g_live.astype(BF16),
            gate_up_tiles[0, 0, 0, 1] * g_live.astype(BF16),
            down_tiles[0, 0, 0] * d_live.astype(BF16),
        ],
        axis=1,
    )
    w = lax.all_gather(own, "tile")

    up_pairs = [(s, (s + 1) % sections) for s in range(sections)]
    down_pairs = [(s, (s - 1) % sections) for s in range(sections)]
    asked = lax.ppermute(tab, "pipe", up_pairs)
    [picked] = call(
        partial(pick_kernel, n), [out_vmem((n, tok, B), BF16)], [], [asked, pending], 8
    )
    cot = lax.ppermute(picked, "pipe", down_pairs)

    coef, h_saved, y = call(
        partial(forward_kernel, n),
        [
            out_vmem((n, tok, 2 * B), F32),
            out_vmem((n + 1, tok, B), BF16),
            out_hbm((1, tok, width), BF16),
        ],
        [
            pltpu.VMEM((n, 2 * tok, 2 * B), F32),
            pltpu.VMEM((n + 1, tok, B), BF16),
            pltpu.VMEM((blocks, tok, B), F32),
        ],
        [tab, x_next, x_saved, w],
        24,
    )
    parts, d_gu = call(
        partial(backward_kernel, n),
        [out_vmem((n, B, 3 * B), BF16), out_vmem((n, tok, 2 * B), BF16)],
        [pltpu.VMEM((n + 1, tok, B), F32)],
        [tab, x_saved, w, coef, h_saved, cot],
        24,
    )
    got = lax.all_to_all(parts, "tile", 0, 0, tiled=True)
    [dx] = call(
        partial(dx_kernel, n),
        [out_hbm((1, tok, width), BF16)],
        [pltpu.VMEM((blocks, tok, B), F32)],
        [tab, d_gu, w],
        24,
    )
    grad_gu, grad_down = call(
        partial(total_kernel, n),
        [out_hbm((1, 1, 1, 2, B, B), F32), out_hbm((1, 1, 1, B, B), F32)],
        [],
        [live, got],
        24,
    )
    return (y, dx, grad_gu, grad_down)


def solution(mesh):
    placed = (
        P("pipe", "tile", None),
        P("pipe", "tile", None),
        P("pipe", "tile", None),
        P("pipe", None, None),
        P("pipe", None, None),
        P("pipe", None),
        P("pipe", None, None),
        P("pipe", None, None),
        P("pipe", None),
        P("pipe", "tile", None, None, None, None),
        P("pipe", "tile", None, None, None),
    )
    return jax.shard_map(
        per_device,
        mesh=mesh,
        in_specs=placed,
        out_specs=(
            P("pipe", "tile", None),
            P("pipe", "tile", None),
            P("pipe", "tile", None, None, None, None),
            P("pipe", "tile", None, None, None),
        ),
        check_vma=False,
    )
```

```python
import functools

import jax
import jax.numpy as jnp
from jax import lax
from jax.experimental import pallas as pl
from jax.experimental.pallas import tpu as pltpu
from jax.sharding import PartitionSpec as P

B = 128
SIDE = 4
CHIPS = SIDE * SIDE
F32 = jnp.float32
BF16 = jnp.bfloat16
ROWS, LEAD, FIRST, HSLOT, DCOLS, OWNER = range(6)


def pairs(first, second, core=0):
    out = []
    for x in range(SIDE):
        for y in range(SIDE):
            for c in range(2):
                dx, dy = (second, first) if c else (first, second)
                to = ((x + dx) % SIDE) * SIDE + (y + dy) % SIDE
                out.append(((x * SIDE + y) * 2 + c, to * 2 + (c + core) % 2))
    return out


def send(value, first, second, core=0):
    return lax.ppermute(value, "tile", pairs(first, second, core))


def gather_tiles(own):
    own = own[None]
    one, three, two = send(own, 1, 0), send(own, -1, 0), send(own, 2, 0)
    near = jnp.concatenate([own, one, two, three], axis=0)
    back, ahead = send(near, 0, 1), send(near, 0, -1)
    low, high = send(back[:2], 0, 1), send(ahead[2:], 0, -1)
    mine = [near, back, low, high, ahead]
    return jnp.concatenate(mine + [send(part, 0, 0, 1) for part in mine], axis=0)


def reduce_tiles(mine, others):
    def plus(a, b):
        return (a.astype(F32) + b.astype(F32)).astype(BF16)

    held = (mine + send(others, 0, 0, 1).astype(F32)).astype(BF16)
    held = held.reshape(SIDE, SIDE, B, 3 * B)
    low, high = send(held[2, :2], 0, -1), send(held[2, 2:], 0, 1)
    to_back = jnp.concatenate([plus(held[1, :2], low), held[1, 2:]], axis=0)
    to_ahead = jnp.concatenate([held[3, :2], plus(held[3, 2:], high)], axis=0)
    from_ahead, from_back = send(to_back, 0, -1), send(to_ahead, 0, 1)
    row = held[0].astype(F32) + from_ahead.astype(F32) + from_back.astype(F32)
    out = row[1:].astype(BF16)
    parts = send(out[0], -1, 0), send(out[1], 2, 0), send(out[2], 1, 0)
    return row[0] + sum(part.astype(F32) for part in parts)


def loop(count, unroll, body):
    def group(i, carry):
        body([i * unroll + u for u in range(unroll)])
        return carry

    lax.fori_loop(0, count // unroll, group, 0)


def cols(block_index):
    return pl.ds(pl.multiple_of(block_index * B, B), B)


def rounded(value):
    return value.astype(BF16).astype(F32)


def dot(a, b, contract_a=1, contract_b=0):
    return lax.dot_general(
        a, b, (((contract_a,), (contract_b,)), ((), ())), preferred_element_type=F32
    )


SMEM, VMEM = pltpu.SMEM, pltpu.VMEM


def kept(shape, dtype):
    return pltpu.VMEM(shape, dtype)


def call(body, outs, scratch, scalars, arrays, limit, flops):
    return pl.pallas_call(
        body,
        out_shape=outs,
        in_specs=[pl.BlockSpec(memory_space=SMEM) for _ in scalars]
        + [pl.BlockSpec(memory_space=VMEM) for _ in arrays],
        out_specs=[pl.BlockSpec(memory_space=VMEM) for _ in outs],
        scratch_shapes=scratch,
        compiler_params=pltpu.CompilerParams(vmem_limit_bytes=limit << 20),
        cost_estimate=pl.CostEstimate(flops=flops, bytes_accessed=4 << 20, transcendentals=0),
    )(*scalars, *[pltpu.with_memory_space_constraint(a, VMEM) for a in arrays])


def pack_kernel(g_live, d_live, mine, tiles, down, out):
    o = mine[0]
    g = jnp.where(g_live[0, o] > 0, 1.0, 0.0)
    d = jnp.where(d_live[0, o] > 0, 1.0, 0.0)
    out[:, :B] = (tiles[0, 0, 0, 0].astype(F32) * g).astype(BF16)
    out[:, B : 2 * B] = (tiles[0, 0, 0, 1].astype(F32) * g).astype(BF16)
    out[:, 2 * B :] = (down[0, 0, 0].astype(F32) * d).astype(BF16)


def pick_kernel(n, asked, pending, out):
    for k in range(n):
        out[k] = pending[0, :, cols(asked[0, k])]


def saved_kernel(n, tab, x_saved, out, turned):
    for k in range(n):
        x = x_saved[0, :, cols(tab[ROWS, k])]
        out[k] = x
        turned[k] = x.T


def project(n, tab, x_of, w, acc):
    def some(ks):
        parts = [rounded(dot(x_of(k), w[k, :, : 2 * B])) for k in ks]
        for k, part in zip(ks, parts):
            lead = tab[LEAD, k]
            acc[lead] = jnp.where(tab[FIRST, k] == 1, part, acc[lead] + part)

    loop(n, 4, some)


def forward_saved_kernel(n, tab, x, w, coef, h_turned, acc):
    project(n, tab, lambda k: x[k], w, acc)

    def activate(ks):
        for k in ks:

            @pl.when(tab[FIRST, k] == 1)
            def _():
                gate, up = acc[k, :, :B], acc[k, :, B:]
                sig = jax.nn.sigmoid(gate)
                act = gate * sig
                h_turned[k] = (act * up).astype(BF16).T
                coef[k, :, :B] = up * sig * (1.0 + gate * (1.0 - sig))
                coef[k, :, B:] = act

    loop(n, 1, activate)
    h_turned[n] = jnp.zeros((B, B), BF16)


def forward_next_kernel(n, tab, x_next, w, y, acc, h, y_acc):
    project(n, tab, lambda k: x_next[0, :, cols(tab[ROWS, k])], w, acc)

    def activate(ks):
        for k in ks:

            @pl.when(tab[FIRST, k] == 1)
            def _():
                gate, up = acc[k, :, :B], acc[k, :, B:]
                h[k] = (gate * jax.nn.sigmoid(gate) * up).astype(BF16)

    loop(n, 1, activate)
    h[n] = jnp.zeros((B, B), BF16)
    y_acc[...] = jnp.zeros_like(y_acc)

    def down(js):
        parts = [rounded(dot(h[tab[HSLOT, j]], w[j, :, 2 * B :])) for j in js]
        for j, part in zip(js, parts):
            y_acc[tab[DCOLS, j]] += part

    loop(n, 4, down)
    for c in range(y_acc.shape[0]):
        y[0, :, c * B : (c + 1) * B] = y_acc[c].astype(BF16)


def backward_kernel(n, tab, x_turned, w, coef, h_turned, cot, mine, others, d_gu, dh):
    half = n // 2
    dh[...] = jnp.zeros_like(dh)

    def down(js):
        parts = [dot(cot[tab[OWNER, j]], w[j, :, 2 * B :], 1, 1) for j in js]
        for j, part in zip(js, parts):
            dh[tab[HSLOT, j]] += rounded(part)

    loop(n, 4, down)

    def scale(ks):
        for k in ks:

            @pl.when(tab[FIRST, k] == 1)
            def _():
                d_gu[k, :, :B] = (dh[k] * coef[k, :, :B]).astype(BF16)
                d_gu[k, :, B:] = (dh[k] * coef[k, :, B:]).astype(BF16)

    loop(n, 1, scale)

    def grads(base, out):
        def some(ks):
            for k in ks:
                s = base + k
                gu = dot(x_turned[s], d_gu[tab[LEAD, s]])
                down = dot(h_turned[tab[HSLOT, s]], cot[tab[OWNER, s]])
                out[k, :, : 2 * B] = gu.astype(out.dtype)
                out[k, :, 2 * B :] = down.astype(out.dtype)

        loop(half, 4, some)

    grads(half, others)
    grads(0, mine)


def dx_kernel(n, tab, d_gu, w, dx, acc):
    acc[...] = jnp.zeros_like(acc)

    def back(ks):
        parts = [rounded(dot(d_gu[tab[LEAD, k]], w[k, :, : 2 * B], 1, 1)) for k in ks]
        for k, part in zip(ks, parts):
            acc[tab[ROWS, k]] += part

    loop(n, 4, back)
    for c in range(acc.shape[0]):
        dx[0, :, c * B : (c + 1) * B] = acc[c].astype(BF16)


def tables(mine, g_rows, g_cols, d_rows, d_cols):
    n = g_rows.shape[0]
    ids = jnp.arange(n, dtype=jnp.int32)
    kind = (ids // CHIPS + mine) % 2
    j, i = (ids // SIDE) % SIDE, ids % SIDE
    x = (mine // (2 * SIDE) - jnp.where(kind == 0, i, j)) % SIDE
    y = ((mine // 2) % SIDE - jnp.where(kind == 0, j, i)) % SIDE
    owner = (x * SIDE + y) * 2 + kind
    chosen = owner[:, None] == ids[None, :]

    def by_slot(values):
        return jnp.sum(jnp.where(chosen, values[None, :], 0), axis=1)

    rows, columns = by_slot(g_rows), by_slot(g_cols)
    lead = jnp.min(jnp.where(columns[:, None] == columns[None, :], ids[None, :], n), axis=1)
    first = (lead == ids).astype(jnp.int32)
    hslot = jnp.min(jnp.where(by_slot(d_rows)[:, None] == columns[None, :], ids[None, :], n), axis=1)
    return jnp.stack([rows, lead, first, hslot, by_slot(d_cols), owner])


def per_device(
    x_next,
    x_saved,
    pending,
    gu_rows,
    gu_cols,
    gu_live,
    down_rows,
    down_cols,
    down_live,
    gate_up_tiles,
    down_tiles,
):
    n = lax.axis_size("tile")
    sections = lax.axis_size("pipe")
    mine = lax.axis_index("tile").astype(jnp.int32)
    tok, width = x_next.shape[1:]
    blocks = width // B
    part = functools.partial
    product = 2 * tok * B * B

    up_pairs = [(s, (s + 1) % sections) for s in range(sections)]
    down_pairs = [(s, (s - 1) % sections) for s in range(sections)]
    d_cols = down_cols[0].reshape(1, n)
    asked = lax.ppermute(d_cols, "pipe", up_pairs)

    [own] = call(
        pack_kernel,
        [kept((B, 3 * B), BF16)],
        [],
        [gu_live, down_live, mine[None]],
        [gate_up_tiles, down_tiles],
        2,
        product,
    )
    w = gather_tiles(own)

    [picked] = call(
        part(pick_kernel, n), [kept((n, tok, B), BF16)], [], [asked], [pending], 4, n * product
    )
    cot = lax.ppermute(picked, "pipe", down_pairs)

    tab = tables(
        mine, gu_rows[0].reshape(-1), gu_cols[0].reshape(-1), down_rows[0].reshape(-1), d_cols.reshape(-1)
    )
    x_blocks, x_turned = call(
        part(saved_kernel, n),
        [kept((n, tok, B), BF16), kept((n, B, tok), BF16)],
        [],
        [tab],
        [x_saved],
        4,
        2 * n * product,
    )
    coef, h_turned = call(
        part(forward_saved_kernel, n),
        [kept((n, tok, 2 * B), F32), kept((n + 1, B, tok), BF16)],
        [VMEM((n, tok, 2 * B), F32)],
        [tab],
        [x_blocks, w],
        10,
        3 * n * product,
    )
    partial_mine, partial_others, d_gu = call(
        part(backward_kernel, n),
        [kept((CHIPS, B, 3 * B), F32), kept((CHIPS, B, 3 * B), BF16), kept((n, tok, 2 * B), BF16)],
        [VMEM((n + 1, tok, B), F32)],
        [tab],
        [x_turned, w, coef, h_turned, cot],
        8,
        5 * n * product,
    )
    x_late, partial_mine = lax.optimization_barrier((x_next, partial_mine))
    total = reduce_tiles(partial_mine, partial_others)
    [y] = call(
        part(forward_next_kernel, n),
        [jax.ShapeDtypeStruct((1, tok, width), BF16)],
        [
            VMEM((n, tok, 2 * B), F32),
            VMEM((n + 1, tok, B), BF16),
            VMEM((blocks, tok, B), F32),
        ],
        [tab],
        [x_late, w],
        20,
        5 * n * product,
    )
    [dx] = call(
        part(dx_kernel, n),
        [jax.ShapeDtypeStruct((1, tok, width), BF16)],
        [VMEM((blocks, tok, B), F32)],
        [tab],
        [d_gu, w],
        10,
        4 * n * product,
    )
    g_live = (lax.dynamic_index_in_dim(gu_live[0], mine, 0, keepdims=False) > 0).astype(F32)
    d_live = (lax.dynamic_index_in_dim(down_live[0], mine, 0, keepdims=False) > 0).astype(F32)
    grad_gu = jnp.stack([total[:, :B], total[:, B : 2 * B]]) * g_live
    grad_down = total[:, 2 * B :] * d_live
    return (y, dx, grad_gu[None, None, None], grad_down[None, None, None])


def solution(mesh):
    placed = (
        P("pipe", "tile", None),
        P("pipe", "tile", None),
        P("pipe", "tile", None),
        P("pipe", None, None),
        P("pipe", None, None),
        P("pipe", None),
        P("pipe", None, None),
        P("pipe", None, None),
        P("pipe", None),
        P("pipe", "tile", None, None, None, None),
        P("pipe", "tile", None, None, None),
    )
    return jax.shard_map(
        per_device,
        mesh=mesh,
        in_specs=placed,
        out_specs=(
            P("pipe", "tile", None),
            P("pipe", "tile", None),
            P("pipe", "tile", None, None, None, None),
            P("pipe", "tile", None, None, None),
        ),
        check_vma=False,
    )
```

```python
import functools

import jax
import jax.numpy as jnp
from jax import lax
from jax.experimental import pallas as pl
from jax.experimental.pallas import tpu as pltpu
from jax.sharding import PartitionSpec as P

B = 128
SIDE = 4
CHIPS = SIDE * SIDE
F32 = jnp.float32
BF16 = jnp.bfloat16
UNROLL = 16
ROWS, LEAD, FIRST, HSLOT, DCOLS, OWNER, GLIVE, DLIVE = range(8)


def pairs(first, second, core=0):
    out = []
    for x in range(SIDE):
        for y in range(SIDE):
            for c in range(2):
                dx, dy = (second, first) if c else (first, second)
                to = ((x + dx) % SIDE) * SIDE + (y + dy) % SIDE
                out.append(((x * SIDE + y) * 2 + c, to * 2 + (c + core) % 2))
    return out


def send(value, first, second, core=0):
    return lax.ppermute(value, "tile", pairs(first, second, core))


def together(*values):
    return lax.optimization_barrier(values)


def gather_tiles(own, cot, late):
    own = own[None]
    one, three, two = send(own, 1, 0), send(own, -1, 0), send(own, 2, 0)
    near = jnp.concatenate([own, one, two, three], axis=0)
    back, ahead = send(near, 0, 1), send(near, 0, -1)
    ahead, late = together(ahead, late)
    low, high = send(back[:2], 0, 1), send(ahead[2:], 0, -1)
    mine = [near, back, low, high, ahead]
    others = [send(part, 0, 0, 1) for part in mine]
    near, cot, *others = together(near, cot, *others)
    return jnp.concatenate([near] + mine[1:] + others, axis=0), cot, late


def plus(a, b):
    return (a.astype(F32) + b.astype(F32)).astype(BF16)


def loop(count, unroll, body):
    def group(i, carry):
        body([i * unroll + u for u in range(unroll)])
        return carry

    lax.fori_loop(0, count // unroll, group, 0)


def cols(block_index):
    return pl.ds(pl.multiple_of(block_index * B, B), B)


def live(tab, row, slot):
    return tab[row, slot].astype(F32)


def rounded(value):
    return value.astype(BF16).astype(F32)


def dot(a, b, contract_a=1, contract_b=0):
    return lax.dot_general(
        a, b, (((contract_a,), (contract_b,)), ((), ())), preferred_element_type=F32
    )


SMEM, VMEM = pltpu.SMEM, pltpu.VMEM


def kept(shape, dtype):
    return pltpu.VMEM(shape, dtype)


def call(body, outs, scratch, scalars, arrays, limit, flops, far=()):
    return pl.pallas_call(
        body,
        out_shape=outs,
        in_specs=[pl.BlockSpec(memory_space=SMEM) for _ in scalars]
        + [pl.BlockSpec(memory_space=pltpu.HBM) for _ in far]
        + [pl.BlockSpec(memory_space=VMEM) for _ in arrays],
        out_specs=[pl.BlockSpec(memory_space=VMEM) for _ in outs],
        scratch_shapes=scratch,
        compiler_params=pltpu.CompilerParams(vmem_limit_bytes=limit << 20),
        cost_estimate=pl.CostEstimate(flops=flops, bytes_accessed=4 << 20, transcendentals=0),
    )(*scalars, *[pltpu.with_memory_space_constraint(a, pltpu.HBM) for a in far], *[pltpu.with_memory_space_constraint(a, VMEM) for a in arrays])


def pick(n, source, table, row, out, sems):
    return [
        pltpu.make_async_copy(source.at[0, :, cols(table[row, k])], out.at[k], sems.at[k])
        for k in range(n)
    ]


def pick_kernel(n, asked, pending, out, sems):
    copies = pick(n, pending, asked, 0, out, sems)
    for copy in copies:
        copy.start()
    for copy in copies:
        copy.wait()


def saved_kernel(n, tab, x_saved, out, turned, sems):
    copies = pick(n, x_saved, tab, ROWS, out, sems)
    for copy in copies:
        copy.start()
    for k, copy in enumerate(copies):
        copy.wait()
        turned[k] = out[k].T


def project(n, tab, x, w, acc):
    def some(ks):
        parts = [rounded(dot(x[k], w[k, :, : 2 * B]) * live(tab, GLIVE, k)) for k in ks]
        for k, part in zip(ks, parts):
            lead = tab[LEAD, k]
            acc[lead] = jnp.where(tab[FIRST, k] == 1, part, acc[lead] + part)

    loop(n, UNROLL, some)


def forward_saved_kernel(n, tab, x, w, coef, h_turned, acc):
    project(n, tab, x, w, acc)

    def activate(ks):
        for k in ks:
            gate, up = acc[k, :, :B], acc[k, :, B:]
            sig = jax.nn.sigmoid(gate)
            act = gate * sig
            h_turned[k] = (act * up).astype(BF16).T
            coef[k, :, :B] = up * sig * (1.0 + gate * (1.0 - sig))
            coef[k, :, B:] = act

    loop(n, 4, activate)
    h_turned[n] = jnp.zeros((B, B), BF16)


def forward_next_kernel(n, tab, x_next, w, h, acc, x, sems):
    copies = pick(n, x_next, tab, ROWS, x, sems)
    for copy in copies:
        copy.start()
    for copy in copies:
        copy.wait()
    project(n, tab, x, w, acc)

    def activate(ks):
        for k in ks:
            gate, up = acc[k, :, :B], acc[k, :, B:]
            h[k] = (gate * jax.nn.sigmoid(gate) * up).astype(BF16)

    loop(n, 4, activate)
    h[n] = jnp.zeros((B, B), BF16)


def down_next_kernel(n, tab, h, w, y, acc):
    acc[...] = jnp.zeros_like(acc)

    def down(js):
        parts = [rounded(dot(h[tab[HSLOT, j]], w[j, :, 2 * B :]) * live(tab, DLIVE, j)) for j in js]
        for j, part in zip(js, parts):
            acc[tab[DCOLS, j]] += part

    loop(n, UNROLL, down)
    for c in range(acc.shape[0]):
        y[0, :, c * B : (c + 1) * B] = acc[c].astype(BF16)


def grads(tab, base, count, x_turned, h_turned, d_gu, cot, out):
    def some(ks):
        for k in ks:
            s = base + k
            gu = dot(x_turned[s], d_gu[tab[LEAD, s]]) * live(tab, GLIVE, s)
            down = dot(h_turned[tab[HSLOT, s]], cot[tab[OWNER, s]]) * live(tab, DLIVE, s)
            out[k, :, : 2 * B] = gu.astype(out.dtype)
            out[k, :, 2 * B :] = down.astype(out.dtype)

    loop(count, UNROLL, some)


def backward_kernel(n, tab, x_turned, w, coef, h_turned, cot, others, d_gu, dh):
    dh[...] = jnp.zeros_like(dh)

    def down(js):
        parts = [dot(cot[tab[OWNER, j]], w[j, :, 2 * B :], 1, 1) * live(tab, DLIVE, j) for j in js]
        for j, part in zip(js, parts):
            dh[tab[HSLOT, j]] += rounded(part)

    loop(n, UNROLL, down)

    def scale(ks):
        for k in ks:
            d_gu[k, :, :B] = (dh[k] * coef[k, :, :B]).astype(BF16)
            d_gu[k, :, B:] = (dh[k] * coef[k, :, B:]).astype(BF16)

    loop(n, 4, scale)
    grads(tab, n // 2, n // 2, x_turned, h_turned, d_gu, cot, others)


def own_grads_kernel(n, tab, x_turned, h_turned, d_gu, cot, mine):
    grads(tab, 0, n // 2, x_turned, h_turned, d_gu, cot, mine)


def dx_kernel(n, tab, d_gu, w, dx, acc):
    acc[...] = jnp.zeros_like(acc)

    def back(ks):
        parts = [
            rounded(dot(d_gu[tab[LEAD, k]], w[k, :, : 2 * B], 1, 1) * live(tab, GLIVE, k)) for k in ks
        ]
        for k, part in zip(ks, parts):
            acc[tab[ROWS, k]] += part

    loop(n, UNROLL, back)
    for c in range(acc.shape[0]):
        dx[0, :, c * B : (c + 1) * B] = acc[c].astype(BF16)


def total_kernel(row, one, two, three, grad_gu, grad_down):
    total = row[...] + (one[...].astype(F32) + two[...].astype(F32) + three[...].astype(F32))
    grad_gu[0, 0, 0, 0] = total[:, :B]
    grad_gu[0, 0, 0, 1] = total[:, B : 2 * B]
    grad_down[0, 0, 0] = total[:, 2 * B :]


def tables(mine, g_rows, g_cols, g_live, d_rows, d_cols, d_live):
    n = g_rows.shape[0]
    ids = jnp.arange(n, dtype=jnp.int32)
    kind = (ids // CHIPS + mine) % 2
    j, i = (ids // SIDE) % SIDE, ids % SIDE
    x = (mine // (2 * SIDE) - jnp.where(kind == 0, i, j)) % SIDE
    y = ((mine // 2) % SIDE - jnp.where(kind == 0, j, i)) % SIDE
    owner = (x * SIDE + y) * 2 + kind
    chosen = owner[:, None] == ids[None, :]

    def by_slot(values):
        return jnp.sum(jnp.where(chosen, values[None, :], 0), axis=1)

    rows, columns = by_slot(g_rows), by_slot(g_cols)
    lead = jnp.min(jnp.where(columns[:, None] == columns[None, :], ids[None, :], n), axis=1)
    first = (lead == ids).astype(jnp.int32)
    hslot = jnp.min(jnp.where(by_slot(d_rows)[:, None] == columns[None, :], ids[None, :], n), axis=1)
    g_on, d_on = ((by_slot(v) > 0).astype(jnp.int32) for v in (g_live, d_live))
    return jnp.stack([rows, lead, first, hslot, by_slot(d_cols), owner, g_on, d_on])


def per_device(
    x_next,
    x_saved,
    pending,
    gu_rows,
    gu_cols,
    gu_live,
    down_rows,
    down_cols,
    down_live,
    gate_up_tiles,
    down_tiles,
):
    n = lax.axis_size("tile")
    sections = lax.axis_size("pipe")
    mine = lax.axis_index("tile").astype(jnp.int32)
    tok, width = x_next.shape[1:]
    blocks = width // B
    part = functools.partial
    product = 2 * tok * B * B

    up_pairs = [(s, (s + 1) % sections) for s in range(sections)]
    down_pairs = [(s, (s - 1) % sections) for s in range(sections)]
    asked = lax.ppermute(down_cols[0].reshape(1, n), "pipe", up_pairs)
    [picked] = call(
        part(pick_kernel, n),
        [kept((n, tok, B), BF16)],
        [pltpu.SemaphoreType.DMA((n,))],
        [asked],
        [],
        2,
        n * product,
        [pending],
    )
    own = jnp.concatenate(
        [gate_up_tiles[0, 0, 0, 0], gate_up_tiles[0, 0, 0, 1], down_tiles[0, 0, 0]], axis=1
    )
    cot = lax.ppermute(picked, "pipe", down_pairs)
    w, cot, x_saved = gather_tiles(own, cot, x_saved)

    tab = tables(
        mine,
        gu_rows[0].reshape(-1),
        gu_cols[0].reshape(-1),
        gu_live[0],
        down_rows[0].reshape(-1),
        down_cols[0].reshape(-1),
        down_live[0],
    )
    x_blocks, x_turned = call(
        part(saved_kernel, n),
        [kept((n, tok, B), BF16), kept((n, B, tok), BF16)],
        [pltpu.SemaphoreType.DMA((n,))],
        [tab],
        [],
        2,
        2 * n * product,
        [x_saved],
    )
    coef, h_turned = call(
        part(forward_saved_kernel, n),
        [kept((n, tok, 2 * B), F32), kept((n + 1, B, tok), BF16)],
        [VMEM((n, tok, 2 * B), F32)],
        [tab],
        [x_blocks, w],
        8,
        3 * n * product,
    )
    others, d_gu = call(
        part(backward_kernel, n),
        [kept((CHIPS, B, 3 * B), BF16), kept((n, tok, 2 * B), BF16)],
        [VMEM((n + 1, tok, B), F32)],
        [tab],
        [x_turned, w, coef, h_turned, cot],
        6,
        4 * n * product,
    )
    arrived = send(others, 0, 0, 1)
    [own_part] = call(
        part(own_grads_kernel, n),
        [kept((CHIPS, B, 3 * B), F32)],
        [],
        [tab],
        [x_turned, h_turned, d_gu, cot],
        4,
        2 * n * product,
    )
    held = plus(own_part, arrived).reshape(SIDE, SIDE, B, 3 * B)
    held, d_gu = together(held, d_gu)
    [dx] = call(
        part(dx_kernel, n),
        [jax.ShapeDtypeStruct((1, tok, width), BF16)],
        [VMEM((blocks, tok, B), F32)],
        [tab],
        [d_gu, w],
        10,
        4 * n * product,
    )
    low, high = send(held[2, :2], 0, -1), send(held[2, 2:], 0, 1)
    low, high, dx = together(low, high, dx)
    to_back = jnp.concatenate([plus(held[1, :2], low), held[1, 2:]], axis=0)
    to_ahead = jnp.concatenate([held[3, :2], plus(held[3, 2:], high)], axis=0)
    to_back, to_ahead, x_next = together(to_back, to_ahead, x_next)
    [h_next] = call(
        part(forward_next_kernel, n),
        [kept((n + 1, tok, B), BF16)],
        [VMEM((n, tok, 2 * B), F32), VMEM((n, tok, B), BF16), pltpu.SemaphoreType.DMA((n,))],
        [tab],
        [w],
        9,
        4 * n * product,
        [x_next],
    )
    from_ahead, from_back = send(to_back, 0, -1), send(to_ahead, 0, 1)
    from_ahead, from_back, h_next = together(from_ahead, from_back, h_next)
    row = held[0].astype(F32) + from_ahead.astype(F32) + from_back.astype(F32)
    row, h_next = together(row, h_next)
    [y] = call(
        part(down_next_kernel, n),
        [jax.ShapeDtypeStruct((1, tok, width), BF16)],
        [VMEM((blocks, tok, B), F32)],
        [tab],
        [h_next, w],
        10,
        4 * n * product,
    )
    out = row[1:].astype(BF16)
    one, two, three = send(out[0], -1, 0), send(out[1], 2, 0), send(out[2], 1, 0)
    one, two, three, y = together(one, two, three, y)
    grad_gu, grad_down = call(
        total_kernel,
        [
            jax.ShapeDtypeStruct((1, 1, 1, 2, B, B), F32),
            jax.ShapeDtypeStruct((1, 1, 1, B, B), F32),
        ],
        [],
        [],
        [row[0], one, two, three],
        2,
        product,
    )
    return (y, dx, grad_gu, grad_down)


def solution(mesh):
    placed = (
        P("pipe", "tile", None),
        P("pipe", "tile", None),
        P("pipe", "tile", None),
        P("pipe", None, None),
        P("pipe", None, None),
        P("pipe", None),
        P("pipe", None, None),
        P("pipe", None, None),
        P("pipe", None),
        P("pipe", "tile", None, None, None, None),
        P("pipe", "tile", None, None, None),
    )
    return jax.shard_map(
        per_device,
        mesh=mesh,
        in_specs=placed,
        out_specs=(
            P("pipe", "tile", None),
            P("pipe", "tile", None),
            P("pipe", "tile", None, None, None, None),
            P("pipe", "tile", None, None, None),
        ),
        check_vma=False,
    )
```

```python
import functools

import jax
import jax.numpy as jnp
from jax import lax
from jax.experimental import pallas as pl
from jax.experimental.pallas import tpu as pltpu
from jax.sharding import PartitionSpec as P

B = 128
SIDE = 4
CHIPS = SIDE * SIDE
F32 = jnp.float32
BF16 = jnp.bfloat16
UNROLL = 16
ROWS, LEAD, FIRST, HSLOT, DCOLS, OWNER, GLIVE, DLIVE = range(8)


def pairs(first, second, core=0):
    out = []
    for x in range(SIDE):
        for y in range(SIDE):
            for c in range(2):
                dx, dy = (second, first) if c else (first, second)
                to = ((x + dx) % SIDE) * SIDE + (y + dy) % SIDE
                out.append(((x * SIDE + y) * 2 + c, to * 2 + (c + core) % 2))
    return out


def send(value, first, second, core=0):
    return lax.ppermute(value, "tile", pairs(first, second, core))


def together(*values):
    return lax.optimization_barrier(values)


def gather_tiles(own, busy):
    own = own[None]
    one, three, two = send(own, 1, 0), send(own, -1, 0), send(own, 2, 0)
    near = jnp.concatenate([own, one, two, three], axis=0)
    back, ahead = send(near, 0, 1), send(near, 0, -1)
    back, ahead, *busy = together(back, ahead, *busy)
    low, high = send(back[:2], 0, 1), send(ahead[2:], 0, -1)
    mine = [near, back, low, high, ahead]
    return mine + [send(part, 0, 0, 1) for part in mine], busy


def plus(a, b):
    return (a.astype(F32) + b.astype(F32)).astype(BF16)


def loop(count, unroll, body):
    def group(i, carry):
        body([i * unroll + u for u in range(unroll)])
        return carry

    lax.fori_loop(0, count // unroll, group, 0)


def flat(count, unroll, body):
    for i in range(0, count, unroll):
        body(list(range(i, i + unroll)))


def cols(block_index):
    return pl.ds(pl.multiple_of(block_index * B, B), B)


def live(tab, row, slot):
    return tab[row, slot].astype(F32)


def rounded(value):
    return value.astype(BF16).astype(F32)


def dot(a, b, contract_a=1, contract_b=0):
    return lax.dot_general(
        a, b, (((contract_a,), (contract_b,)), ((), ())), preferred_element_type=F32
    )


SMEM, VMEM = pltpu.SMEM, pltpu.VMEM


def kept(shape, dtype):
    return pltpu.VMEM(shape, dtype)


def call(body, outs, scratch, scalars, arrays, limit, flops=0, far=(), out_space=VMEM):
    return pl.pallas_call(
        body,
        out_shape=outs,
        in_specs=[pl.BlockSpec(memory_space=SMEM) for _ in scalars]
        + [pl.BlockSpec(memory_space=pltpu.HBM) for _ in far]
        + [pl.BlockSpec(memory_space=VMEM) for _ in arrays],
        out_specs=[pl.BlockSpec(memory_space=out_space) for _ in outs],
        scratch_shapes=scratch,
        compiler_params=pltpu.CompilerParams(vmem_limit_bytes=limit << 20),
        cost_estimate=pl.CostEstimate(flops=flops, bytes_accessed=flops // 256, transcendentals=0),
    )(*scalars, *[pltpu.with_memory_space_constraint(a, pltpu.HBM) for a in far], *[pltpu.with_memory_space_constraint(a, VMEM) for a in arrays])


def pick(n, source, table, row, out, sems):
    return [
        pltpu.make_async_copy(source.at[0, :, cols(table[row, k])], out.at[k], sems.at[k])
        for k in range(n)
    ]


def pack_kernel(gate_up, down, out, sems):
    copies = [
        pltpu.make_async_copy(gate_up.at[0, 0, 0], out.at[pl.ds(0, 2)], sems.at[0]),
        pltpu.make_async_copy(down.at[0, 0, 0], out.at[2], sems.at[1]),
    ]
    for copy in copies:
        copy.start()
    for copy in copies:
        copy.wait()


def pick_kernel(n, asked, pending, out, sems):
    copies = pick(n, pending, asked, 0, out, sems)
    for copy in copies:
        copy.start()
    for copy in copies:
        copy.wait()


def saved_kernel(n, tab, x_saved, out, turned, sems):
    copies = pick(n, x_saved, tab, ROWS, out, sems)
    for copy in copies:
        copy.start()
    for k, copy in enumerate(copies):
        copy.wait()
        turned[k] = out[k].T


def project(n, tab, x, w_of, acc, walk):
    def some(ks):
        parts = [rounded(dot(x[k], w_of(k)) * live(tab, GLIVE, k)) for k in ks]
        for k, part in zip(ks, parts):
            lead = tab[LEAD, k]
            acc[lead] = jnp.where(tab[FIRST, k] == 1, part, acc[lead] + part)

    walk(n, UNROLL, some)


def forward_saved_kernel(n, tab, x, *refs):
    *pieces, w, coef, h_turned, acc = refs
    places = [(piece, i) for piece in pieces for i in range(piece.shape[0])]

    def w_of(k):
        piece, i = places[k]
        gate, up = piece[i, 0], piece[i, 1]
        w[k, :, :B], w[k, :, B : 2 * B], w[k, :, 2 * B :] = gate, up, piece[i, 2]
        return jnp.concatenate([gate, up], axis=1)

    project(n, tab, x, w_of, acc, flat)

    def activate(ks):
        for k in ks:
            gate, up = acc[k, :, :B], acc[k, :, B:]
            sig = jax.nn.sigmoid(gate)
            act = gate * sig
            h_turned[k] = (act * up).astype(BF16).T
            coef[k, :, :B] = up * sig * (1.0 + gate * (1.0 - sig))
            coef[k, :, B:] = act

    loop(n, 4, activate)
    h_turned[n] = jnp.zeros((B, B), BF16)


def forward_next_kernel(n, tab, x_next, w, h, acc, x, sems):
    copies = pick(n, x_next, tab, ROWS, x, sems)
    for copy in copies:
        copy.start()
    for copy in copies:
        copy.wait()
    project(n, tab, x, lambda k: w[k, :, : 2 * B], acc, loop)

    def activate(ks):
        for k in ks:
            gate, up = acc[k, :, :B], acc[k, :, B:]
            h[k] = (gate * jax.nn.sigmoid(gate) * up).astype(BF16)

    loop(n, 4, activate)
    h[n] = jnp.zeros((B, B), BF16)


def put(acc, out, staged, sems):
    chunks = sems.shape[0]
    each = acc.shape[0] // chunks
    copies = []
    for q in range(chunks):
        for c in range(q * each, (q + 1) * each):
            staged[:, c * B : (c + 1) * B] = acc[c].astype(BF16)
        span = pl.ds(q * each * B, each * B)
        copy = pltpu.make_async_copy(staged.at[:, span], out.at[0, :, span], sems.at[q])
        copy.start()
        copies.append(copy)
    for copy in copies:
        copy.wait()


def down_next_kernel(n, tab, h, w, y, acc, staged, sems):
    acc[...] = jnp.zeros_like(acc)

    def down(js):
        parts = [rounded(dot(h[tab[HSLOT, j]], w[j, :, 2 * B :]) * live(tab, DLIVE, j)) for j in js]
        for j, part in zip(js, parts):
            acc[tab[DCOLS, j]] += part

    loop(n, UNROLL, down)
    put(acc, y, staged, sems)


def grads(tab, slots, x_turned, h_turned, d_gu, cot, out):
    for k, s in enumerate(slots):
        gu = dot(x_turned[s], d_gu[tab[LEAD, s]]) * live(tab, GLIVE, s)
        down = dot(h_turned[tab[HSLOT, s]], cot[tab[OWNER, s]]) * live(tab, DLIVE, s)
        out[k, :, : 2 * B] = gu.astype(out.dtype)
        out[k, :, 2 * B :] = down.astype(out.dtype)


def backward_kernel(n, slots, tab, x_turned, w, coef, h_turned, cot, others, own, d_gu, dh):
    dh[...] = jnp.zeros_like(dh)

    def down(js):
        parts = [dot(cot[tab[OWNER, j]], w[j, :, 2 * B :], 1, 1) * live(tab, DLIVE, j) for j in js]
        for j, part in zip(js, parts):
            dh[tab[HSLOT, j]] += rounded(part)

    loop(n, UNROLL, down)

    def scale(ks):
        for k in ks:
            d_gu[k, :, :B] = (dh[k] * coef[k, :, :B]).astype(BF16)
            d_gu[k, :, B:] = (dh[k] * coef[k, :, B:]).astype(BF16)

    loop(n, 4, scale)
    for some, out in zip(slots, (others, own)):
        grads(tab, some, x_turned, h_turned, d_gu, cot, out)


def grads_kernel(slots, tab, x_turned, h_turned, d_gu, cot, *outs):
    for some, out in zip(slots, outs):
        grads(tab, some, x_turned, h_turned, d_gu, cot, out)


def dx_kernel(n, tab, d_gu, w, dx, acc, staged, sems):
    acc[...] = jnp.zeros_like(acc)

    def back(ks):
        parts = [
            rounded(dot(d_gu[tab[LEAD, k]], w[k, :, : 2 * B], 1, 1) * live(tab, GLIVE, k)) for k in ks
        ]
        for k, part in zip(ks, parts):
            acc[tab[ROWS, k]] += part

    loop(n, UNROLL, back)
    put(acc, dx, staged, sems)


def total_kernel(row, one, two, three, grad_gu, grad_down):
    total = row[...] + (one[...].astype(F32) + two[...].astype(F32) + three[...].astype(F32))
    grad_gu[0, 0, 0, 0] = total[:, :B]
    grad_gu[0, 0, 0, 1] = total[:, B : 2 * B]
    grad_down[0, 0, 0] = total[:, 2 * B :]


def tables(mine, g_rows, g_cols, g_live, d_rows, d_cols, d_live):
    n = g_rows.shape[0]
    ids = jnp.arange(n, dtype=jnp.int32)
    kind = (ids // CHIPS + mine) % 2
    j, i = (ids // SIDE) % SIDE, ids % SIDE
    x = (mine // (2 * SIDE) - jnp.where(kind == 0, i, j)) % SIDE
    y = ((mine // 2) % SIDE - jnp.where(kind == 0, j, i)) % SIDE
    owner = (x * SIDE + y) * 2 + kind
    chosen = owner[:, None] == ids[None, :]

    def by_slot(values):
        return jnp.sum(jnp.where(chosen, values[None, :], 0), axis=1)

    rows, columns = by_slot(g_rows), by_slot(g_cols)
    lead = jnp.min(jnp.where(columns[:, None] == columns[None, :], ids[None, :], n), axis=1)
    first = (lead == ids).astype(jnp.int32)
    hslot = jnp.min(jnp.where(by_slot(d_rows)[:, None] == columns[None, :], ids[None, :], n), axis=1)
    g_on, d_on = ((by_slot(v) > 0).astype(jnp.int32) for v in (g_live, d_live))
    return jnp.stack([rows, lead, first, hslot, by_slot(d_cols), owner, g_on, d_on])


def per_device(
    x_next,
    x_saved,
    pending,
    gu_rows,
    gu_cols,
    gu_live,
    down_rows,
    down_cols,
    down_live,
    gate_up_tiles,
    down_tiles,
):
    n = lax.axis_size("tile")
    sections = lax.axis_size("pipe")
    mine = lax.axis_index("tile").astype(jnp.int32)
    tok, width = x_next.shape[1:]
    blocks = width // B
    part = functools.partial
    product = 2 * tok * B * B

    up_pairs = [(s, (s + 1) % sections) for s in range(sections)]
    down_pairs = [(s, (s - 1) % sections) for s in range(sections)]
    asked = lax.ppermute(down_cols[0].reshape(1, n), "pipe", up_pairs)
    [picked] = call(
        part(pick_kernel, n),
        [kept((n, tok, B), BF16)],
        [pltpu.SemaphoreType.DMA((n,))],
        [asked],
        [],
        2,
        far=[pending],
    )
    cot = lax.ppermute(picked, "pipe", down_pairs)

    tab = tables(
        mine,
        gu_rows[0].reshape(-1),
        gu_cols[0].reshape(-1),
        gu_live[0],
        down_rows[0].reshape(-1),
        down_cols[0].reshape(-1),
        down_live[0],
    )
    x_blocks, x_turned = call(
        part(saved_kernel, n),
        [kept((n, tok, B), BF16), kept((n, B, tok), BF16)],
        [pltpu.SemaphoreType.DMA((n,))],
        [tab],
        [],
        2,
        far=[x_saved],
    )
    [own] = call(
        pack_kernel,
        [kept((3, B, B), BF16)],
        [pltpu.SemaphoreType.DMA((2,))],
        [],
        [],
        2,
        far=[gate_up_tiles, down_tiles],
    )
    pieces, (x_blocks, x_turned) = gather_tiles(own, [x_blocks, x_turned])
    w, coef, h_turned = call(
        part(forward_saved_kernel, n),
        [kept((n, B, 3 * B), BF16), kept((n, tok, 2 * B), F32), kept((n + 1, B, tok), BF16)],
        [VMEM((n, tok, 2 * B), F32)],
        [tab],
        [x_blocks, *pieces],
        8,
    )
    ring = [[4 * j + i for i in range(SIDE)] for j in range(SIDE)]
    late_slots = ring[1] + ring[3] + ring[0]
    other_first, own_first, d_gu = call(
        part(backward_kernel, n, [[CHIPS + k for k in ring[2]], ring[2]]),
        [
            kept((SIDE, B, 3 * B), BF16),
            kept((SIDE, B, 3 * B), F32),
            kept((n, tok, 2 * B), BF16),
        ],
        [VMEM((n + 1, tok, B), F32)],
        [tab],
        [x_turned, w, coef, h_turned, cot],
        6,
    )
    first = send(other_first, 0, 0, 1)
    [other_late] = call(
        part(grads_kernel, [[CHIPS + k for k in late_slots]]),
        [kept((CHIPS - SIDE, B, 3 * B), BF16)],
        [],
        [tab],
        [x_turned, h_turned, d_gu, cot],
        4,
    )
    late = send(other_late, 0, 0, 1)
    held = plus(own_first, first)
    low, high = send(held[:2], 0, -1), send(held[2:], 0, 1)
    [own_late] = call(
        part(grads_kernel, [late_slots]),
        [kept((CHIPS - SIDE, B, 3 * B), F32)],
        [],
        [tab],
        [x_turned, h_turned, d_gu, cot],
        4,
    )
    both = (own_late + late.astype(F32)).reshape(SIDE - 1, SIDE, B, 3 * B)
    both, d_gu = together(both, d_gu)
    [dx] = call(
        part(dx_kernel, n),
        [jax.ShapeDtypeStruct((1, tok, width), BF16)],
        [VMEM((blocks, tok, B), F32), VMEM((tok, width), BF16), pltpu.SemaphoreType.DMA((4,))],
        [tab],
        [d_gu, w],
        8,
        4 * n * product,
        out_space=pltpu.HBM,
    )
    low, high, dx = together(low, high, dx)
    to_back = jnp.concatenate([plus(both[0, :2], low), both[0, 2:].astype(BF16)], axis=0)
    to_ahead = jnp.concatenate([both[1, :2].astype(BF16), plus(both[1, 2:], high)], axis=0)
    to_back, to_ahead, x_next = together(to_back, to_ahead, x_next)
    [h_next] = call(
        part(forward_next_kernel, n),
        [kept((n + 1, tok, B), BF16)],
        [VMEM((n, tok, 2 * B), F32), VMEM((n, tok, B), BF16), pltpu.SemaphoreType.DMA((n,))],
        [tab],
        [w],
        9,
        4 * n * product,
        [x_next],
    )
    from_ahead, from_back = send(to_back, 0, -1), send(to_ahead, 0, 1)
    from_ahead, from_back, h_next = together(from_ahead, from_back, h_next)
    row = both[2] + from_ahead.astype(F32) + from_back.astype(F32)
    row, h_next = together(row, h_next)
    [y] = call(
        part(down_next_kernel, n),
        [jax.ShapeDtypeStruct((1, tok, width), BF16)],
        [VMEM((blocks, tok, B), F32), VMEM((tok, width), BF16), pltpu.SemaphoreType.DMA((4,))],
        [tab],
        [h_next, w],
        8,
        4 * n * product,
        out_space=pltpu.HBM,
    )
    out = row[1:].astype(BF16)
    one, two, three = send(out[0], -1, 0), send(out[1], 2, 0), send(out[2], 1, 0)
    one, two, three, y = together(one, two, three, y)
    grad_gu, grad_down = call(
        total_kernel,
        [
            jax.ShapeDtypeStruct((1, 1, 1, 2, B, B), F32),
            jax.ShapeDtypeStruct((1, 1, 1, B, B), F32),
        ],
        [],
        [],
        [row[0], one, two, three],
        2,
        product,
    )
    return (y, dx, grad_gu, grad_down)


def solution(mesh):
    placed = (
        P("pipe", "tile", None),
        P("pipe", "tile", None),
        P("pipe", "tile", None),
        P("pipe", None, None),
        P("pipe", None, None),
        P("pipe", None),
        P("pipe", None, None),
        P("pipe", None, None),
        P("pipe", None),
        P("pipe", "tile", None, None, None, None),
        P("pipe", "tile", None, None, None),
    )
    return jax.shard_map(
        per_device,
        mesh=mesh,
        in_specs=placed,
        out_specs=(
            P("pipe", "tile", None),
            P("pipe", "tile", None),
            P("pipe", "tile", None, None, None, None),
            P("pipe", "tile", None, None, None),
        ),
        check_vma=False,
    )
```

```python
import functools

import jax
import jax.numpy as jnp
from jax import lax
from jax.experimental import pallas as pl
from jax.experimental.pallas import tpu as pltpu
from jax.sharding import PartitionSpec as P

B = 128
SIDE = 4
CHIPS = SIDE * SIDE
F32 = jnp.float32
BF16 = jnp.bfloat16
UNROLL = 16
ROWS, LEAD, FIRST, HSLOT, DCOLS, OWNER, GLIVE, DLIVE = range(8)

OTHER = (0, 0, 0, 1, 0, 1, 1, 1)
STEPS = (0, 1, 3, 0, 2, 1, 3, 2)


def group(other, j):
    [g] = [g for g in range(len(STEPS)) if (OTHER[g], STEPS[g]) == (other, j)]
    return [g * SIDE + i for i in range(SIDE)]


def pairs(first, second, core=0):
    out = []
    for x in range(SIDE):
        for y in range(SIDE):
            for c in range(2):
                dx, dy = (second, first) if c else (first, second)
                to = ((x + dx) % SIDE) * SIDE + (y + dy) % SIDE
                out.append(((x * SIDE + y) * 2 + c, to * 2 + (c + core) % 2))
    return out


def send(value, first, second, core=0):
    return lax.ppermute(value, "tile", pairs(first, second, core))


def together(*values):
    return lax.optimization_barrier(values)


def core(value):
    return send(value, 0, 0, 1)


def plus(a, b):
    return (a.astype(F32) + b.astype(F32)).astype(BF16)


def loop(count, unroll, body):
    def group(i, carry):
        body([i * unroll + u for u in range(unroll)])
        return carry

    lax.fori_loop(0, count // unroll, group, 0)


def cols(block_index):
    return pl.ds(pl.multiple_of(block_index * B, B), B)


def live(tab, row, slot):
    return tab[row, slot].astype(F32)


def rounded(value):
    return value.astype(BF16).astype(F32)


def dot(a, b, contract_a=1, contract_b=0):
    return lax.dot_general(
        a, b, (((contract_a,), (contract_b,)), ((), ())), preferred_element_type=F32
    )


SMEM, VMEM = pltpu.SMEM, pltpu.VMEM


def kept(shape, dtype):
    return pltpu.VMEM(shape, dtype)


def call(body, outs, scratch, scalars, arrays, limit, flops=0, far=(), out_space=VMEM, aliases={}):
    return pl.pallas_call(
        body,
        out_shape=outs,
        in_specs=[pl.BlockSpec(memory_space=SMEM) for _ in scalars]
        + [pl.BlockSpec(memory_space=pltpu.HBM) for _ in far]
        + [pl.BlockSpec(memory_space=VMEM) for _ in arrays],
        out_specs=[pl.BlockSpec(memory_space=out_space) for _ in outs],
        scratch_shapes=scratch,
        input_output_aliases=aliases,
        compiler_params=pltpu.CompilerParams(vmem_limit_bytes=limit << 20),
        cost_estimate=pl.CostEstimate(flops=flops, bytes_accessed=flops // 256, transcendentals=0),
    )(*scalars, *[pltpu.with_memory_space_constraint(a, pltpu.HBM) for a in far], *[pltpu.with_memory_space_constraint(a, VMEM) for a in arrays])


def pack_kernel(gate_up, down, out, sems):
    copies = [
        pltpu.make_async_copy(gate_up.at[0, 0, 0], out.at[pl.ds(0, 2)], sems.at[0]),
        pltpu.make_async_copy(down.at[0, 0, 0], out.at[2], sems.at[1]),
    ]
    for copy in copies:
        copy.start()
    for copy in copies:
        copy.wait()


def fetch_kernel(source, out, sem):
    copy = pltpu.make_async_copy(source.at[0], out, sem)
    copy.start()
    copy.wait()


def pick_kernel(n, asked, pending, out):
    for k in range(n):
        out[k] = pending[:, cols(asked[0, k])]


def saved_kernel(n, tab, x_saved, out, turned, x, sem):
    fetch_kernel(x_saved, x, sem)
    for k in range(n):
        block = x[:, cols(tab[ROWS, k])]
        out[k] = block
        turned[k] = block.T


def project(tab, slots, x_of, w_of, acc):
    parts = [rounded(dot(x_of(k), w_of(k)) * live(tab, GLIVE, k)) for k in slots]
    for k, part in zip(slots, parts):
        lead = tab[LEAD, k]
        acc[lead] = jnp.where(tab[FIRST, k] == 1, part, acc[lead] + part)


def project_pieces(tab, start, x, pieces, w, acc):
    places = [(piece, i) for piece in pieces for i in range(piece.shape[0])]

    def w_of(k):
        piece, i = places[k - start]
        gate, up = piece[i, 0], piece[i, 1]
        w[k, :, :B], w[k, :, B : 2 * B], w[k, :, 2 * B :] = gate, up, piece[i, 2]
        return jnp.concatenate([gate, up], axis=1)

    project(tab, range(start, start + len(places)), lambda k: x[k], w_of, acc)


def saved_first_kernel(tab, x, *refs):
    *pieces, w, acc = refs
    project_pieces(tab, 0, x, pieces, w, acc)


def saved_more_kernel(start, tab, x, *refs):
    *pieces, _, _, w, acc = refs
    project_pieces(tab, start, x, pieces, w, acc)


def saved_last_kernel(n, start, tab, x, *refs):
    *pieces, _, _, w, acc, coef, h_turned = refs
    project_pieces(tab, start, x, pieces, w, acc)

    def activate(ks):
        for k in ks:
            gate, up = acc[k, :, :B], acc[k, :, B:]
            sig = jax.nn.sigmoid(gate)
            act = gate * sig
            h_turned[k] = (act * up).astype(BF16).T
            coef[k, :, :B] = up * sig * (1.0 + gate * (1.0 - sig))
            coef[k, :, B:] = act

    loop(n, 4, activate)
    h_turned[n] = jnp.zeros((B, B), BF16)


def forward_next_kernel(n, tab, x_next, w, h, acc, x, sem):
    fetch_kernel(x_next, x, sem)

    def some(ks):
        project(tab, ks, lambda k: x[:, cols(tab[ROWS, k])], lambda k: w[k, :, : 2 * B], acc)

    loop(n, UNROLL, some)

    def activate(ks):
        for k in ks:
            gate, up = acc[k, :, :B], acc[k, :, B:]
            h[k] = (gate * jax.nn.sigmoid(gate) * up).astype(BF16)

    loop(n, 4, activate)
    h[n] = jnp.zeros((B, B), BF16)


def put(acc, out, staged, sems):
    chunks = sems.shape[0]
    each = acc.shape[0] // chunks
    copies = []
    for q in range(chunks):
        for c in range(q * each, (q + 1) * each):
            staged[:, c * B : (c + 1) * B] = acc[c].astype(BF16)
        span = pl.ds(q * each * B, each * B)
        copy = pltpu.make_async_copy(staged.at[:, span], out.at[0, :, span], sems.at[q])
        copy.start()
        copies.append(copy)
    for copy in copies:
        copy.wait()


def down_next_kernel(n, tab, h, w, y, acc, staged, sems):
    acc[...] = jnp.zeros_like(acc)

    def down(js):
        parts = [rounded(dot(h[tab[HSLOT, j]], w[j, :, 2 * B :]) * live(tab, DLIVE, j)) for j in js]
        for j, part in zip(js, parts):
            acc[tab[DCOLS, j]] += part

    loop(n, UNROLL, down)
    put(acc, y, staged, sems)


def grads(tab, slots, x_turned, h_turned, d_gu, cot, out):
    for k, s in enumerate(slots):
        gu = dot(x_turned[s], d_gu[tab[LEAD, s]]) * live(tab, GLIVE, s)
        down = dot(h_turned[tab[HSLOT, s]], cot[tab[OWNER, s]]) * live(tab, DLIVE, s)
        out[k, :, : 2 * B] = gu.astype(out.dtype)
        out[k, :, 2 * B :] = down.astype(out.dtype)


def backward_kernel(n, slots, tab, x_turned, w, coef, h_turned, cot, others, own, d_gu, dh):
    dh[...] = jnp.zeros_like(dh)

    def down(js):
        parts = [dot(cot[tab[OWNER, j]], w[j, :, 2 * B :], 1, 1) * live(tab, DLIVE, j) for j in js]
        for j, part in zip(js, parts):
            dh[tab[HSLOT, j]] += rounded(part)

    loop(n, UNROLL, down)

    def scale(ks):
        for k in ks:
            d_gu[k, :, :B] = (dh[k] * coef[k, :, :B]).astype(BF16)
            d_gu[k, :, B:] = (dh[k] * coef[k, :, B:]).astype(BF16)

    loop(n, 4, scale)
    for some, out in zip(slots, (others, own)):
        grads(tab, some, x_turned, h_turned, d_gu, cot, out)


def grads_kernel(slots, tab, x_turned, h_turned, d_gu, cot, *outs):
    for some, out in zip(slots, outs):
        grads(tab, some, x_turned, h_turned, d_gu, cot, out)


def dx_kernel(n, tab, d_gu, w, dx, acc, staged, sems):
    acc[...] = jnp.zeros_like(acc)

    def back(ks):
        parts = [
            rounded(dot(d_gu[tab[LEAD, k]], w[k, :, : 2 * B], 1, 1) * live(tab, GLIVE, k)) for k in ks
        ]
        for k, part in zip(ks, parts):
            acc[tab[ROWS, k]] += part

    loop(n, UNROLL, back)
    put(acc, dx, staged, sems)


def total_kernel(row, one, two, three, grad_gu, grad_down):
    total = row[...] + (one[...].astype(F32) + two[...].astype(F32) + three[...].astype(F32))
    grad_gu[0, 0, 0, 0] = total[:, :B]
    grad_gu[0, 0, 0, 1] = total[:, B : 2 * B]
    grad_down[0, 0, 0] = total[:, 2 * B :]


def tables(mine, g_rows, g_cols, g_live, d_rows, d_cols, d_live):
    n = g_rows.shape[0]
    ids = jnp.arange(n, dtype=jnp.int32)
    kind = (jnp.repeat(jnp.array(OTHER, jnp.int32), SIDE) + mine) % 2
    j, i = jnp.repeat(jnp.array(STEPS, jnp.int32), SIDE), ids % SIDE
    x = (mine // (2 * SIDE) - jnp.where(kind == 0, i, j)) % SIDE
    y = ((mine // 2) % SIDE - jnp.where(kind == 0, j, i)) % SIDE
    owner = (x * SIDE + y) * 2 + kind
    chosen = owner[:, None] == ids[None, :]

    def by_slot(values):
        return jnp.sum(jnp.where(chosen, values[None, :], 0), axis=1)

    rows, columns = by_slot(g_rows), by_slot(g_cols)
    lead = jnp.min(jnp.where(columns[:, None] == columns[None, :], ids[None, :], n), axis=1)
    first = (lead == ids).astype(jnp.int32)
    hslot = jnp.min(jnp.where(by_slot(d_rows)[:, None] == columns[None, :], ids[None, :], n), axis=1)
    g_on, d_on = ((by_slot(v) > 0).astype(jnp.int32) for v in (g_live, d_live))
    return jnp.stack([rows, lead, first, hslot, by_slot(d_cols), owner, g_on, d_on])


def per_device(
    x_next,
    x_saved,
    pending,
    gu_rows,
    gu_cols,
    gu_live,
    down_rows,
    down_cols,
    down_live,
    gate_up_tiles,
    down_tiles,
):
    n = lax.axis_size("tile")
    sections = lax.axis_size("pipe")
    mine = lax.axis_index("tile").astype(jnp.int32)
    tok, width = x_next.shape[1:]
    blocks = width // B
    part = functools.partial
    product = 2 * tok * B * B

    up_pairs = [(s, (s + 1) % sections) for s in range(sections)]
    down_pairs = [(s, (s - 1) % sections) for s in range(sections)]
    asked = lax.ppermute(down_cols[0].reshape(1, n), "pipe", up_pairs)
    one_copy = [pltpu.SemaphoreType.DMA]
    [held_back] = call(fetch_kernel, [kept((tok, width), BF16)], one_copy, [], [], 2, far=[pending])
    [picked] = call(
        part(pick_kernel, n), [kept((n, tok, B), BF16)], [], [asked], [held_back], 2
    )
    cot = lax.ppermute(picked, "pipe", down_pairs)

    [own] = call(
        pack_kernel,
        [kept((3, B, B), BF16)],
        [pltpu.SemaphoreType.DMA((2,))],
        [],
        [],
        2,
        far=[gate_up_tiles, down_tiles],
    )
    own = own[None]
    one, three, two = send(own, 1, 0), send(own, -1, 0), send(own, 2, 0)
    near = jnp.concatenate([own, one, two, three], axis=0)
    near, gu_rows, gu_cols, down_rows = together(near, gu_rows, gu_cols, down_rows)
    back, ahead = send(near, 0, 1), send(near, 0, -1)
    near_core = core(near)

    tab = tables(
        mine,
        gu_rows[0].reshape(-1),
        gu_cols[0].reshape(-1),
        gu_live[0],
        down_rows[0].reshape(-1),
        down_cols[0].reshape(-1),
        down_live[0],
    )
    x_blocks, x_turned = call(
        part(saved_kernel, n),
        [kept((n, tok, B), BF16), kept((n, B, tok), BF16)],
        [VMEM((tok, width), BF16), *one_copy],
        [tab],
        [],
        4,
        far=[x_saved],
    )
    back, ahead, x_blocks, x_turned = together(back, ahead, x_blocks, x_turned)
    low, high = send(back[:2], 0, 1), send(ahead[2:], 0, -1)
    tiles, gates = kept((n, B, 3 * B), BF16), kept((n, tok, 2 * B), F32)
    w, acc = call(
        saved_first_kernel, [tiles, gates], [], [tab], [x_blocks, near, back, ahead, near_core], 6
    )
    low, high, w, acc = together(low, high, w, acc)
    more = [low, high, core(back), core(ahead)]
    w, acc = call(
        part(saved_more_kernel, CHIPS),
        [tiles, gates],
        [],
        [tab],
        [x_blocks, *more, w, acc],
        6,
        aliases={6: 0, 7: 1},
    )
    last = [core(low), core(high)]
    w, acc, coef, h_turned = call(
        part(saved_last_kernel, n, n - SIDE),
        [tiles, gates, gates, kept((n + 1, B, tok), BF16)],
        [],
        [tab],
        [x_blocks, *last, w, acc],
        6,
        aliases={4: 0, 5: 1},
    )
    late_steps = (1, 3, 0)
    own_late_slots = sum((group(0, j) for j in late_steps), [])
    other_late_slots = sum((group(1, j) for j in late_steps), [])
    other_first, own_first, d_gu = call(
        part(backward_kernel, n, [group(1, 2), group(0, 2)]),
        [
            kept((SIDE, B, 3 * B), BF16),
            kept((SIDE, B, 3 * B), F32),
            kept((n, tok, 2 * B), BF16),
        ],
        [VMEM((n + 1, tok, B), F32)],
        [tab],
        [x_turned, w, coef, h_turned, cot],
        6,
    )
    first = core(other_first)
    [own_late] = call(
        part(grads_kernel, [own_late_slots]),
        [kept((CHIPS - SIDE, B, 3 * B), F32)],
        [],
        [tab],
        [x_turned, h_turned, d_gu, cot],
        4,
    )
    held = plus(own_first, first)
    held, own_late, d_gu = together(held, own_late, d_gu)
    low, high = send(held[:2], 0, -1), send(held[2:], 0, 1)
    [other_late] = call(
        part(grads_kernel, [other_late_slots]),
        [kept((CHIPS - SIDE, B, 3 * B), BF16)],
        [],
        [tab],
        [x_turned, h_turned, d_gu, cot],
        4,
    )
    late = core(other_late)
    both = (own_late + late.astype(F32)).reshape(SIDE - 1, SIDE, B, 3 * B)
    [dx] = call(
        part(dx_kernel, n),
        [jax.ShapeDtypeStruct((1, tok, width), BF16)],
        [VMEM((blocks, tok, B), F32), VMEM((tok, width), BF16), pltpu.SemaphoreType.DMA((4,))],
        [tab],
        [d_gu, w],
        8,
        4 * n * product,
        out_space=pltpu.HBM,
    )
    low, high, dx = together(low, high, dx)
    to_back = jnp.concatenate([plus(both[0, :2], low), both[0, 2:].astype(BF16)], axis=0)
    to_ahead = jnp.concatenate([both[1, :2].astype(BF16), plus(both[1, 2:], high)], axis=0)
    to_back, to_ahead, x_next = together(to_back, to_ahead, x_next)
    [h_next] = call(
        part(forward_next_kernel, n),
        [kept((n + 1, tok, B), BF16)],
        [VMEM((n, tok, 2 * B), F32), VMEM((tok, width), BF16), *one_copy],
        [tab],
        [w],
        9,
        4 * n * product,
        [x_next],
    )
    from_ahead, from_back = send(to_back, 0, -1), send(to_ahead, 0, 1)
    from_ahead, from_back, h_next = together(from_ahead, from_back, h_next)
    row = both[2] + from_ahead.astype(F32) + from_back.astype(F32)
    row, h_next = together(row, h_next)
    [y] = call(
        part(down_next_kernel, n),
        [jax.ShapeDtypeStruct((1, tok, width), BF16)],
        [VMEM((blocks, tok, B), F32), VMEM((tok, width), BF16), pltpu.SemaphoreType.DMA((4,))],
        [tab],
        [h_next, w],
        8,
        4 * n * product,
        out_space=pltpu.HBM,
    )
    out = row[1:].astype(BF16)
    one, two, three = send(out[0], -1, 0), send(out[1], 2, 0), send(out[2], 1, 0)
    one, two, three, y = together(one, two, three, y)
    grad_gu, grad_down = call(
        total_kernel,
        [
            jax.ShapeDtypeStruct((1, 1, 1, 2, B, B), F32),
            jax.ShapeDtypeStruct((1, 1, 1, B, B), F32),
        ],
        [],
        [],
        [row[0], one, two, three],
        2,
        product,
    )
    return (y, dx, grad_gu, grad_down)


def solution(mesh):
    placed = (
        P("pipe", "tile", None),
        P("pipe", "tile", None),
        P("pipe", "tile", None),
        P("pipe", None, None),
        P("pipe", None, None),
        P("pipe", None),
        P("pipe", None, None),
        P("pipe", None, None),
        P("pipe", None),
        P("pipe", "tile", None, None, None, None),
        P("pipe", "tile", None, None, None),
    )
    return jax.shard_map(
        per_device,
        mesh=mesh,
        in_specs=placed,
        out_specs=(
            P("pipe", "tile", None),
            P("pipe", "tile", None),
            P("pipe", "tile", None, None, None, None),
            P("pipe", "tile", None, None, None),
        ),
        check_vma=False,
    )
```

```python
import functools

import jax
import jax.numpy as jnp
import numpy as np
from jax import lax
from jax.experimental import pallas as pl
from jax.experimental.pallas import tpu as pltpu
from jax.sharding import PartitionSpec as P

B = 128
SIDE = 4
CHIPS = SIDE * SIDE
F32 = jnp.float32
BF16 = jnp.bfloat16
UNROLL = 16
ROWS, LEAD, FIRST, HSLOT, DCOLS, OWNER, GLIVE, DLIVE = range(8)

OTHER = (0, 0, 0, 1, 0, 1, 1, 1)
STEPS = (0, 1, 3, 0, 2, 1, 3, 2)


def group(other, j):
    [g] = [g for g in range(len(STEPS)) if (OTHER[g], STEPS[g]) == (other, j)]
    return [g * SIDE + i for i in range(SIDE)]


def pairs(first, second, core=0):
    out = []
    for x in range(SIDE):
        for y in range(SIDE):
            for c in range(2):
                dx, dy = (second, first) if c else (first, second)
                to = ((x + dx) % SIDE) * SIDE + (y + dy) % SIDE
                out.append(((x * SIDE + y) * 2 + c, to * 2 + (c + core) % 2))
    return out


def send(value, first, second, core=0):
    return lax.ppermute(value, "tile", pairs(first, second, core))


def together(*values):
    return lax.optimization_barrier(values)


def core(value):
    return send(value, 0, 0, 1)


def plus(a, b):
    return (a.astype(F32) + b.astype(F32)).astype(BF16)


def loop(count, unroll, body):
    def group(i, carry):
        body([i * unroll + u for u in range(unroll)])
        return carry

    lax.fori_loop(0, count // unroll, group, 0)


def cols(block_index):
    return pl.ds(pl.multiple_of(block_index * B, B), B)


def live(tab, row, slot):
    return tab[row, slot].astype(F32)


def rounded(value):
    return value.astype(BF16).astype(F32)


def dot(a, b, contract_a=1, contract_b=0):
    return lax.dot_general(
        a, b, (((contract_a,), (contract_b,)), ((), ())), preferred_element_type=F32
    )


SMEM, VMEM = pltpu.SMEM, pltpu.VMEM


def kept(shape, dtype):
    return pltpu.VMEM(shape, dtype)


def call(body, outs, scratch, scalars, arrays, limit, flops=0, far=(), out_space=VMEM, aliases={}):
    return pl.pallas_call(
        body,
        out_shape=outs,
        in_specs=[pl.BlockSpec(memory_space=SMEM) for _ in scalars]
        + [pl.BlockSpec(memory_space=pltpu.HBM) for _ in far]
        + [pl.BlockSpec(memory_space=VMEM) for _ in arrays],
        out_specs=[pl.BlockSpec(memory_space=out_space) for _ in outs],
        scratch_shapes=scratch,
        input_output_aliases=aliases,
        compiler_params=pltpu.CompilerParams(vmem_limit_bytes=limit << 20),
        cost_estimate=pl.CostEstimate(flops=flops, bytes_accessed=flops // 256, transcendentals=0),
    )(*scalars, *[pltpu.with_memory_space_constraint(a, pltpu.HBM) for a in far], *[pltpu.with_memory_space_constraint(a, VMEM) for a in arrays])


def row_copies(source, out, sems):
    count = sems.shape[0]
    each = out.shape[0] // count
    rows = [pl.ds(q * each, each) for q in range(count)]
    return [pltpu.make_async_copy(source.at[0, r], out.at[r], sems.at[q]) for q, r in enumerate(rows)]


def pack_kernel(gate_up, down, pending, out, held, sems, row_sems):
    copies = [
        pltpu.make_async_copy(gate_up.at[0, 0, 0], out.at[pl.ds(0, 2)], sems.at[0]),
        pltpu.make_async_copy(down.at[0, 0, 0], out.at[2], sems.at[1]),
        *row_copies(pending, held, row_sems),
    ]
    for copy in copies:
        copy.start()
    for copy in copies:
        copy.wait()


def pick_kernel(n, asked, pending, out):
    for k in range(n):
        out[k] = pending[:, cols(asked[0, k])]


def saved_kernel(n, tab, x_saved, x_next, out, turned, later, x, sems, later_sems):
    now, then = row_copies(x_saved, x, sems), row_copies(x_next, later, later_sems)
    for copy in now + then:
        copy.start()
    for copy in now:
        copy.wait()
    for k in range(n):
        block = x[:, cols(tab[ROWS, k])]
        out[k] = block
        turned[k] = block.T
    for copy in then:
        copy.wait()


def project(tab, slots, x_of, w_of, acc):
    parts = [rounded(dot(x_of(k), w_of(k)) * live(tab, GLIVE, k)) for k in slots]
    for k, part in zip(slots, parts):
        lead = tab[LEAD, k]
        acc[lead] = jnp.where(tab[FIRST, k] == 1, part, acc[lead] + part)


def project_pieces(tab, start, x, pieces, w, acc):
    places = [(piece, i) for piece in pieces for i in range(piece.shape[0])]

    def w_of(k):
        piece, i = places[k - start]
        gate, up = piece[i, 0], piece[i, 1]
        w[k, :, :B], w[k, :, B : 2 * B], w[k, :, 2 * B :] = gate, up, piece[i, 2]
        return jnp.concatenate([gate, up], axis=1)

    project(tab, range(start, start + len(places)), lambda k: x[k], w_of, acc)


def saved_first_kernel(tab, x, *refs):
    *pieces, w, acc = refs
    project_pieces(tab, 0, x, pieces, w, acc)


def saved_more_kernel(start, tab, x, *refs):
    *pieces, _, _, w, acc = refs
    project_pieces(tab, start, x, pieces, w, acc)


def saved_last_kernel(n, start, tab, x, *refs):
    *pieces, _, _, w, acc, coef, h_turned = refs
    project_pieces(tab, start, x, pieces, w, acc)

    def activate(ks):
        for k in ks:
            gate, up = acc[k, :, :B], acc[k, :, B:]
            sig = jax.nn.sigmoid(gate)
            act = gate * sig
            h_turned[k] = (act * up).astype(BF16).T
            coef[k, :, :B] = up * sig * (1.0 + gate * (1.0 - sig))
            coef[k, :, B:] = act

    loop(n, 4, activate)
    h_turned[n] = jnp.zeros((B, B), BF16)


def put(acc, out, staged, sems):
    chunks = sems.shape[0]
    each = acc.shape[0] // chunks
    copies = []
    for q in range(chunks):
        for c in range(q * each, (q + 1) * each):
            staged[:, c * B : (c + 1) * B] = acc[c].astype(BF16)
        span = pl.ds(q * each * B, each * B)
        copy = pltpu.make_async_copy(staged.at[:, span], out.at[0, :, span], sems.at[q])
        copy.start()
        copies.append(copy)
    for copy in copies:
        copy.wait()


def next_kernel(n, tab, x, w, y, acc, h, y_acc, staged, sems):
    def some(ks):
        project(tab, ks, lambda k: x[:, cols(tab[ROWS, k])], lambda k: w[k, :, : 2 * B], acc)

    loop(n, UNROLL, some)

    def activate(ks):
        for k in ks:
            gate, up = acc[k, :, :B], acc[k, :, B:]
            h[k] = (gate * jax.nn.sigmoid(gate) * up).astype(BF16)

    loop(n, 4, activate)
    h[n] = jnp.zeros((B, B), BF16)
    y_acc[...] = jnp.zeros_like(y_acc)

    def down(js):
        parts = [rounded(dot(h[tab[HSLOT, j]], w[j, :, 2 * B :]) * live(tab, DLIVE, j)) for j in js]
        for j, part in zip(js, parts):
            y_acc[tab[DCOLS, j]] += part

    loop(n, UNROLL, down)
    put(y_acc, y, staged, sems)


def grads(tab, slots, x_turned, h_turned, d_gu, cot, out):
    for k, s in enumerate(slots):
        gu = dot(x_turned[s], d_gu[tab[LEAD, s]]) * live(tab, GLIVE, s)
        down = dot(h_turned[tab[HSLOT, s]], cot[tab[OWNER, s]]) * live(tab, DLIVE, s)
        out[k, :, : 2 * B] = gu.astype(out.dtype)
        out[k, :, 2 * B :] = down.astype(out.dtype)


def backward_kernel(n, slots, tab, x_turned, w, coef, h_turned, cot, others, d_gu, dh):
    dh[...] = jnp.zeros_like(dh)

    def down(js):
        parts = [dot(cot[tab[OWNER, j]], w[j, :, 2 * B :], 1, 1) * live(tab, DLIVE, j) for j in js]
        for j, part in zip(js, parts):
            dh[tab[HSLOT, j]] += rounded(part)

    loop(n, UNROLL, down)

    def scale(ks):
        for k in ks:
            d_gu[k, :, :B] = (dh[k] * coef[k, :, :B]).astype(BF16)
            d_gu[k, :, B:] = (dh[k] * coef[k, :, B:]).astype(BF16)

    loop(n, 4, scale)
    grads(tab, slots, x_turned, h_turned, d_gu, cot, others)


def grads_kernel(slots, tab, x_turned, h_turned, d_gu, cot, *outs):
    for some, out in zip(slots, outs):
        grads(tab, some, x_turned, h_turned, d_gu, cot, out)


def dx_kernel(n, tab, d_gu, w, dx, acc, staged, sems):
    acc[...] = jnp.zeros_like(acc)

    def back(ks):
        parts = [
            rounded(dot(d_gu[tab[LEAD, k]], w[k, :, : 2 * B], 1, 1) * live(tab, GLIVE, k)) for k in ks
        ]
        for k, part in zip(ks, parts):
            acc[tab[ROWS, k]] += part

    loop(n, UNROLL, back)
    put(acc, dx, staged, sems)


def total_kernel(row, one, two, three, grad_gu, grad_down):
    total = row[...] + (one[...].astype(F32) + two[...].astype(F32) + three[...].astype(F32))
    grad_gu[0, 0, 0, 0] = total[:, :B]
    grad_gu[0, 0, 0, 1] = total[:, B : 2 * B]
    grad_down[0, 0, 0] = total[:, 2 * B :]


def tables(mine, g_rows, g_cols, g_live, d_rows, d_cols, d_live):
    n = g_rows.shape[0]
    ids = jnp.arange(n, dtype=jnp.int32)
    kind = (np.repeat(np.array(OTHER, np.int32), SIDE) + mine) % 2
    j, i = np.repeat(np.array(STEPS, np.int32), SIDE), ids % SIDE
    x = (mine // (2 * SIDE) - jnp.where(kind == 0, i, j)) % SIDE
    y = ((mine // 2) % SIDE - jnp.where(kind == 0, j, i)) % SIDE
    owner = (x * SIDE + y) * 2 + kind
    chosen = owner[:, None] == ids[None, :]

    def by_slot(values):
        return jnp.sum(jnp.where(chosen, values[None, :], 0), axis=1)

    rows, columns = by_slot(g_rows), by_slot(g_cols)
    lead = jnp.min(jnp.where(columns[:, None] == columns[None, :], ids[None, :], n), axis=1)
    first = (lead == ids).astype(jnp.int32)
    hslot = jnp.min(jnp.where(by_slot(d_rows)[:, None] == columns[None, :], ids[None, :], n), axis=1)
    g_on, d_on = ((by_slot(v) > 0).astype(jnp.int32) for v in (g_live, d_live))
    return jnp.stack([rows, lead, first, hslot, by_slot(d_cols), owner, g_on, d_on])


def per_device(
    x_next,
    x_saved,
    pending,
    gu_rows,
    gu_cols,
    gu_live,
    down_rows,
    down_cols,
    down_live,
    gate_up_tiles,
    down_tiles,
):
    n = lax.axis_size("tile")
    sections = lax.axis_size("pipe")
    mine = lax.axis_index("tile").astype(jnp.int32)
    tok, width = x_next.shape[1:]
    blocks = width // B
    part = functools.partial
    product = 2 * tok * B * B

    up_pairs = [(s, (s + 1) % sections) for s in range(sections)]
    down_pairs = [(s, (s - 1) % sections) for s in range(sections)]
    asked = lax.ppermute(down_cols[0].reshape(1, n), "pipe", up_pairs)
    rows, sems = kept((tok, width), BF16), pltpu.SemaphoreType.DMA
    own, held_back = call(
        pack_kernel,
        [kept((3, B, B), BF16), rows],
        [sems((2,)), sems((8,))],
        [],
        [],
        2,
        far=[gate_up_tiles, down_tiles, pending],
    )
    [picked] = call(
        part(pick_kernel, n), [kept((n, tok, B), BF16)], [], [asked], [held_back], 2
    )
    cot = lax.ppermute(picked, "pipe", down_pairs)

    own = own[None]
    one, three, two = send(own, 1, 0), send(own, -1, 0), send(own, 2, 0)
    near = jnp.concatenate([own, one, two, three], axis=0)
    near, gu_rows, gu_cols, down_rows = together(near, gu_rows, gu_cols, down_rows)
    back, ahead = send(near, 0, 1), send(near, 0, -1)
    near_core = core(near)

    tab = tables(
        mine,
        gu_rows[0].reshape(-1),
        gu_cols[0].reshape(-1),
        gu_live[0],
        down_rows[0].reshape(-1),
        down_cols[0].reshape(-1),
        down_live[0],
    )
    x_blocks, x_turned, x_late = call(
        part(saved_kernel, n),
        [kept((n, tok, B), BF16), kept((n, B, tok), BF16), rows],
        [VMEM((tok, width), BF16), sems((8,)), sems((8,))],
        [tab],
        [],
        4,
        far=[x_saved, x_next],
    )
    back, ahead, x_blocks, x_turned = together(back, ahead, x_blocks, x_turned)
    low, high = send(back[:2], 0, 1), send(ahead[2:], 0, -1)
    tiles, gates = kept((n, B, 3 * B), BF16), kept((n, tok, 2 * B), F32)
    w, acc = call(
        saved_first_kernel, [tiles, gates], [], [tab], [x_blocks, near, back, ahead, near_core], 6
    )
    low, high, w, acc = together(low, high, w, acc)
    more = [low, high, core(back), core(ahead)]
    w, acc = call(
        part(saved_more_kernel, CHIPS),
        [tiles, gates],
        [],
        [tab],
        [x_blocks, *more, w, acc],
        6,
        aliases={6: 0, 7: 1},
    )
    last = [core(low), core(high)]
    w, acc, coef, h_turned = call(
        part(saved_last_kernel, n, n - SIDE),
        [tiles, gates, gates, kept((n + 1, B, tok), BF16)],
        [],
        [tab],
        [x_blocks, *last, w, acc],
        6,
        aliases={4: 0, 5: 1},
    )
    other_first, d_gu = call(
        part(backward_kernel, n, group(1, 2)),
        [kept((SIDE, B, 3 * B), BF16), kept((n, tok, 2 * B), BF16)],
        [VMEM((n + 1, tok, B), F32)],
        [tab],
        [x_turned, w, coef, h_turned, cot],
        6,
    )

    def products(d_gu, *outs):
        return call(
            part(grads_kernel, [slots for slots, _ in outs]),
            [kept((len(slots), B, 3 * B), dtype) for slots, dtype in outs],
            [],
            [tab],
            [x_turned, h_turned, d_gu, cot],
            4,
        )

    first = core(other_first)
    own_first, own_next = products(d_gu, (group(0, 2), F32), (group(0, 1) + group(0, 3), F32))
    held = plus(own_first, first)
    held, own_next, d_gu = together(held, own_next, d_gu)
    low, high = send(held[:2], 0, -1), send(held[2:], 0, 1)
    [other_next] = products(d_gu, (group(1, 1) + group(1, 3), BF16))
    arrived = core(other_next)
    [dx] = call(
        part(dx_kernel, n),
        [jax.ShapeDtypeStruct((1, tok, width), BF16)],
        [VMEM((blocks, tok, B), F32), VMEM((tok, width), BF16), sems((4,))],
        [tab],
        [d_gu, w],
        8,
        4 * n * product,
        out_space=pltpu.HBM,
    )
    low, high, dx, d_gu = together(low, high, dx, d_gu)
    both = (own_next + arrived.astype(F32)).reshape(2, SIDE, B, 3 * B)
    to_back = jnp.concatenate([plus(both[0, :2], low), both[0, 2:].astype(BF16)], axis=0)
    to_ahead = jnp.concatenate([both[1, :2].astype(BF16), plus(both[1, 2:], high)], axis=0)
    to_back, to_ahead, x_late, d_gu = together(to_back, to_ahead, x_late, d_gu)
    from_ahead, from_back = send(to_back, 0, -1), send(to_ahead, 0, 1)
    other_last, own_last = products(d_gu, (group(1, 0), BF16), (group(0, 0), F32))
    last = core(other_last)
    [y] = call(
        part(next_kernel, n),
        [jax.ShapeDtypeStruct((1, tok, width), BF16)],
        [
            VMEM((n, tok, 2 * B), F32),
            VMEM((n + 1, tok, B), BF16),
            VMEM((blocks, tok, B), F32),
            VMEM((tok, width), BF16),
            sems((4,)),
        ],
        [tab],
        [x_late, w],
        14,
        8 * n * product,
        out_space=pltpu.HBM,
    )
    from_ahead, from_back, y = together(from_ahead, from_back, y)
    row = own_last + last.astype(F32) + from_ahead.astype(F32) + from_back.astype(F32)
    out = row[1:].astype(BF16)
    one, two, three = send(out[0], -1, 0), send(out[1], 2, 0), send(out[2], 1, 0)
    grad_gu, grad_down = call(
        total_kernel,
        [
            jax.ShapeDtypeStruct((1, 1, 1, 2, B, B), F32),
            jax.ShapeDtypeStruct((1, 1, 1, B, B), F32),
        ],
        [],
        [],
        [row[0], one, two, three],
        2,
        product,
    )
    return (y, dx, grad_gu, grad_down)


def solution(mesh):
    placed = (
        P("pipe", "tile", None),
        P("pipe", "tile", None),
        P("pipe", "tile", None),
        P("pipe", None, None),
        P("pipe", None, None),
        P("pipe", None),
        P("pipe", None, None),
        P("pipe", None, None),
        P("pipe", None),
        P("pipe", "tile", None, None, None, None),
        P("pipe", "tile", None, None, None),
    )
    return jax.shard_map(
        per_device,
        mesh=mesh,
        in_specs=placed,
        out_specs=(
            P("pipe", "tile", None),
            P("pipe", "tile", None),
            P("pipe", "tile", None, None, None, None),
            P("pipe", "tile", None, None, None),
        ),
        check_vma=False,
    )
```

```python
import functools

import jax
import jax.numpy as jnp
import numpy as np
from jax import lax
from jax.experimental import pallas as pl
from jax.experimental.pallas import tpu as pltpu
from jax.sharding import PartitionSpec as P

B = 128
SIDE = 4
CHIPS = SIDE * SIDE
F32 = jnp.float32
BF16 = jnp.bfloat16
UNROLL = 16
ROWS, LEAD, FIRST, HSLOT, DCOLS, OWNER, GLIVE, DLIVE = range(8)

OTHER = (0, 0, 0, 0, 1, 1, 1, 1)
STEPS = (0, 1, 3, 2, 0, 1, 3, 2)


def group(other, j):
    [g] = [g for g in range(len(STEPS)) if (OTHER[g], STEPS[g]) == (other, j)]
    return [g * SIDE + i for i in range(SIDE)]


def pairs(first, second, core=0):
    out = []
    for x in range(SIDE):
        for y in range(SIDE):
            for c in range(2):
                dx, dy = (second, first) if c else (first, second)
                to = ((x + dx) % SIDE) * SIDE + (y + dy) % SIDE
                out.append(((x * SIDE + y) * 2 + c, to * 2 + (c + core) % 2))
    return out


def send(value, first, second, core=0):
    return lax.ppermute(value, "tile", pairs(first, second, core))


def together(*values):
    return lax.optimization_barrier(values)


def core(value):
    return send(value, 0, 0, 1)


def plus(a, b):
    return (a.astype(F32) + b.astype(F32)).astype(BF16)


def loop(count, unroll, body):
    def group(i, carry):
        body([i * unroll + u for u in range(unroll)])
        return carry

    lax.fori_loop(0, count // unroll, group, 0)


def cols(block_index):
    return pl.ds(pl.multiple_of(block_index * B, B), B)


def live(tab, row, slot):
    return tab[row, slot].astype(F32)


def rounded(value):
    return value.astype(BF16).astype(F32)


def dot(a, b, contract_a=1, contract_b=0):
    return lax.dot_general(
        a, b, (((contract_a,), (contract_b,)), ((), ())), preferred_element_type=F32
    )


SMEM, VMEM = pltpu.SMEM, pltpu.VMEM


def kept(shape, dtype):
    return pltpu.VMEM(shape, dtype)


def call(body, outs, scratch, scalars, arrays, limit, flops=0, far=(), out_space=VMEM, aliases={}):
    return pl.pallas_call(
        body,
        out_shape=outs,
        in_specs=[pl.BlockSpec(memory_space=SMEM) for _ in scalars]
        + [pl.BlockSpec(memory_space=pltpu.HBM) for _ in far]
        + [pl.BlockSpec(memory_space=VMEM) for _ in arrays],
        out_specs=[pl.BlockSpec(memory_space=out_space) for _ in outs],
        scratch_shapes=scratch,
        input_output_aliases=aliases,
        compiler_params=pltpu.CompilerParams(vmem_limit_bytes=limit << 20),
        cost_estimate=pl.CostEstimate(flops=flops, bytes_accessed=flops // 256, transcendentals=0),
    )(*scalars, *[pltpu.with_memory_space_constraint(a, pltpu.HBM) for a in far], *[pltpu.with_memory_space_constraint(a, VMEM) for a in arrays])


def row_copies(source, out, sems):
    count = sems.shape[0]
    each = out.shape[0] // count
    rows = [pl.ds(q * each, each) for q in range(count)]
    return [pltpu.make_async_copy(source.at[0, r], out.at[r], sems.at[q]) for q, r in enumerate(rows)]


def pack_kernel(gate_up, down, pending, out, held, sems, row_sems):
    copies = [
        pltpu.make_async_copy(gate_up.at[0, 0, 0], out.at[pl.ds(0, 2)], sems.at[0]),
        pltpu.make_async_copy(down.at[0, 0, 0], out.at[2], sems.at[1]),
        *row_copies(pending, held, row_sems),
    ]
    for copy in copies:
        copy.start()
    for copy in copies:
        copy.wait()


def pick_kernel(n, asked, pending, out):
    for k in range(n):
        out[k] = pending[:, cols(asked[0, k])]


def saved_kernel(n, tab, x_saved, x_next, out, turned, later, x, sems, later_sems):
    now, then = row_copies(x_saved, x, sems), row_copies(x_next, later, later_sems)
    for copy in now + then:
        copy.start()
    for copy in now:
        copy.wait()
    for k in range(n):
        block = x[:, cols(tab[ROWS, k])]
        out[k] = block
        turned[k] = block.T
    for copy in then:
        copy.wait()


def project(tab, slots, x_of, w_of, acc):
    parts = [rounded(dot(x_of(k), w_of(k)) * live(tab, GLIVE, k)) for k in slots]
    for k, part in zip(slots, parts):
        lead = tab[LEAD, k]
        acc[lead] = jnp.where(tab[FIRST, k] == 1, part, acc[lead] + part)


def project_pieces(tab, start, x, pieces, w, acc):
    places = [(piece, i) for piece in pieces for i in range(piece.shape[0])]

    def w_of(k):
        piece, i = places[k - start]
        gate, up = piece[i, 0], piece[i, 1]
        w[k, :, :B], w[k, :, B : 2 * B], w[k, :, 2 * B :] = gate, up, piece[i, 2]
        return jnp.concatenate([gate, up], axis=1)

    project(tab, range(start, start + len(places)), lambda k: x[k], w_of, acc)


def saved_first_kernel(tab, x, *refs):
    *pieces, w, acc = refs
    project_pieces(tab, 0, x, pieces, w, acc)


def saved_more_kernel(start, tab, x, *refs):
    *pieces, _, _, w, acc = refs
    project_pieces(tab, start, x, pieces, w, acc)


def saved_last_kernel(n, start, tab, x, *refs):
    *pieces, _, _, w, acc, coef, h_turned = refs
    project_pieces(tab, start, x, pieces, w, acc)

    def activate(ks):
        for k in ks:
            gate, up = acc[k, :, :B], acc[k, :, B:]
            sig = jax.nn.sigmoid(gate)
            act = gate * sig
            h_turned[k] = (act * up).astype(BF16).T
            coef[k, :, :B] = up * sig * (1.0 + gate * (1.0 - sig))
            coef[k, :, B:] = act

    loop(n, 4, activate)
    h_turned[n] = jnp.zeros((B, B), BF16)


def put(acc, out, staged, sems):
    chunks = sems.shape[0]
    each = acc.shape[0] // chunks
    copies = []
    for q in range(chunks):
        for c in range(q * each, (q + 1) * each):
            staged[:, c * B : (c + 1) * B] = acc[c].astype(BF16)
        span = pl.ds(q * each * B, each * B)
        copy = pltpu.make_async_copy(staged.at[:, span], out.at[0, :, span], sems.at[q])
        copy.start()
        copies.append(copy)
    for copy in copies:
        copy.wait()


def forward_next_kernel(n, tab, x, w, h, acc):
    def some(ks):
        project(tab, ks, lambda k: x[:, cols(tab[ROWS, k])], lambda k: w[k, :, : 2 * B], acc)

    loop(n, UNROLL, some)

    def activate(ks):
        for k in ks:
            gate, up = acc[k, :, :B], acc[k, :, B:]
            h[k] = (gate * jax.nn.sigmoid(gate) * up).astype(BF16)

    loop(n, 4, activate)
    h[n] = jnp.zeros((B, B), BF16)


def down_next_kernel(n, tab, h, w, y, acc, staged, sems):
    acc[...] = jnp.zeros_like(acc)

    def down(js):
        parts = [rounded(dot(h[tab[HSLOT, j]], w[j, :, 2 * B :]) * live(tab, DLIVE, j)) for j in js]
        for j, part in zip(js, parts):
            acc[tab[DCOLS, j]] += part

    loop(n, UNROLL, down)
    put(acc, y, staged, sems)


def grads(tab, slots, x_turned, h_turned, d_gu, cot, out):
    for k, s in enumerate(slots):
        gu = dot(x_turned[s], d_gu[tab[LEAD, s]]) * live(tab, GLIVE, s)
        down = dot(h_turned[tab[HSLOT, s]], cot[tab[OWNER, s]]) * live(tab, DLIVE, s)
        out[k, :, : 2 * B] = gu.astype(out.dtype)
        out[k, :, 2 * B :] = down.astype(out.dtype)


def backward_kernel(n, slots, tab, x_turned, w, coef, h_turned, cot, others, d_gu, dh):
    dh[...] = jnp.zeros_like(dh)

    def down(js):
        parts = [dot(cot[tab[OWNER, j]], w[j, :, 2 * B :], 1, 1) * live(tab, DLIVE, j) for j in js]
        for j, part in zip(js, parts):
            dh[tab[HSLOT, j]] += rounded(part)

    loop(n, UNROLL, down)

    def scale(ks):
        for k in ks:
            d_gu[k, :, :B] = (dh[k] * coef[k, :, :B]).astype(BF16)
            d_gu[k, :, B:] = (dh[k] * coef[k, :, B:]).astype(BF16)

    loop(n, 4, scale)
    grads(tab, slots, x_turned, h_turned, d_gu, cot, others)


def grads_kernel(slots, tab, x_turned, h_turned, d_gu, cot, *outs):
    for some, out in zip(slots, outs):
        grads(tab, some, x_turned, h_turned, d_gu, cot, out)


def dx_kernel(n, tab, d_gu, w, dx, acc, staged, sems):
    acc[...] = jnp.zeros_like(acc)

    def back(ks):
        parts = [
            rounded(dot(d_gu[tab[LEAD, k]], w[k, :, : 2 * B], 1, 1) * live(tab, GLIVE, k)) for k in ks
        ]
        for k, part in zip(ks, parts):
            acc[tab[ROWS, k]] += part

    loop(n, UNROLL, back)
    put(acc, dx, staged, sems)


def total_kernel(row, one, two, three, grad_gu, grad_down):
    total = row[...] + (one[...].astype(F32) + two[...].astype(F32) + three[...].astype(F32))
    grad_gu[0, 0, 0, 0] = total[:, :B]
    grad_gu[0, 0, 0, 1] = total[:, B : 2 * B]
    grad_down[0, 0, 0] = total[:, 2 * B :]


def tables(mine, g_rows, g_cols, g_live, d_rows, d_cols, d_live):
    n = g_rows.shape[0]
    ids = jnp.arange(n, dtype=jnp.int32)
    kind = (np.repeat(np.array(OTHER, np.int32), SIDE) + mine) % 2
    j, i = np.repeat(np.array(STEPS, np.int32), SIDE), ids % SIDE
    x = (mine // (2 * SIDE) - jnp.where(kind == 0, i, j)) % SIDE
    y = ((mine // 2) % SIDE - jnp.where(kind == 0, j, i)) % SIDE
    owner = (x * SIDE + y) * 2 + kind
    chosen = owner[:, None] == ids[None, :]

    def by_slot(values):
        return jnp.sum(jnp.where(chosen, values[None, :], 0), axis=1)

    rows, columns = by_slot(g_rows), by_slot(g_cols)
    lead = jnp.min(jnp.where(columns[:, None] == columns[None, :], ids[None, :], n), axis=1)
    first = (lead == ids).astype(jnp.int32)
    hslot = jnp.min(jnp.where(by_slot(d_rows)[:, None] == columns[None, :], ids[None, :], n), axis=1)
    g_on, d_on = ((by_slot(v) > 0).astype(jnp.int32) for v in (g_live, d_live))
    return jnp.stack([rows, lead, first, hslot, by_slot(d_cols), owner, g_on, d_on])


def per_device(
    x_next,
    x_saved,
    pending,
    gu_rows,
    gu_cols,
    gu_live,
    down_rows,
    down_cols,
    down_live,
    gate_up_tiles,
    down_tiles,
):
    n = lax.axis_size("tile")
    sections = lax.axis_size("pipe")
    mine = lax.axis_index("tile").astype(jnp.int32)
    tok, width = x_next.shape[1:]
    blocks = width // B
    part = functools.partial
    product = 2 * tok * B * B

    up_pairs = [(s, (s + 1) % sections) for s in range(sections)]
    down_pairs = [(s, (s - 1) % sections) for s in range(sections)]
    asked = lax.ppermute(down_cols[0].reshape(1, n), "pipe", up_pairs)
    rows, sems = kept((tok, width), BF16), pltpu.SemaphoreType.DMA
    own, held_back = call(
        pack_kernel,
        [kept((3, B, B), BF16), rows],
        [sems((2,)), sems((8,))],
        [],
        [],
        2,
        far=[gate_up_tiles, down_tiles, pending],
    )
    own, asked = together(own[None], asked)
    one, three, two = send(own, 1, 0), send(own, -1, 0), send(own, 2, 0)
    [picked] = call(
        part(pick_kernel, n), [kept((n, tok, B), BF16)], [], [asked], [held_back], 2
    )
    cot = lax.ppermute(picked, "pipe", down_pairs)
    near = jnp.concatenate([own, one, two, three], axis=0)
    near, gu_rows, gu_cols, down_rows = together(near, gu_rows, gu_cols, down_rows)
    back, ahead = send(near, 0, 1), send(near, 0, -1)

    tab = tables(
        mine,
        gu_rows[0].reshape(-1),
        gu_cols[0].reshape(-1),
        gu_live[0],
        down_rows[0].reshape(-1),
        down_cols[0].reshape(-1),
        down_live[0],
    )
    x_blocks, x_turned, x_late = call(
        part(saved_kernel, n),
        [kept((n, tok, B), BF16), kept((n, B, tok), BF16), rows],
        [VMEM((tok, width), BF16), sems((8,)), sems((8,))],
        [tab],
        [],
        4,
        far=[x_saved, x_next],
    )
    back, ahead, near, x_blocks, x_turned = together(back, ahead, near, x_blocks, x_turned)
    low, high = send(back[:2], 0, 1), send(ahead[2:], 0, -1)
    tiles, gates = kept((n, B, 3 * B), BF16), kept((n, tok, 2 * B), F32)
    w, acc = call(
        saved_first_kernel, [tiles, gates], [], [tab], [x_blocks, near, back, ahead], 6
    )
    low, high, w, acc = together(low, high, w, acc)
    more = [low, high, core(near), core(back), core(ahead)]
    w, acc = call(
        part(saved_more_kernel, CHIPS - SIDE),
        [tiles, gates],
        [],
        [tab],
        [x_blocks, *more, w, acc],
        6,
        aliases={7: 0, 8: 1},
    )
    last = [core(low), core(high)]
    w, acc, coef, h_turned = call(
        part(saved_last_kernel, n, n - SIDE),
        [tiles, gates, gates, kept((n + 1, B, tok), BF16)],
        [],
        [tab],
        [x_blocks, *last, w, acc],
        6,
        aliases={4: 0, 5: 1},
    )
    other_first, d_gu = call(
        part(backward_kernel, n, group(1, 2)),
        [kept((SIDE, B, 3 * B), BF16), kept((n, tok, 2 * B), BF16)],
        [VMEM((n + 1, tok, B), F32)],
        [tab],
        [x_turned, w, coef, h_turned, cot],
        6,
    )

    def products(d_gu, *outs):
        return call(
            part(grads_kernel, [slots for slots, _ in outs]),
            [kept((len(slots), B, 3 * B), dtype) for slots, dtype in outs],
            [],
            [tab],
            [x_turned, h_turned, d_gu, cot],
            4,
        )

    first = core(other_first)
    own_first, own_next = products(d_gu, (group(0, 2), F32), (group(0, 1) + group(0, 3), F32))
    held = plus(own_first, first)
    held, own_next, d_gu = together(held, own_next, d_gu)
    low, high = send(held[:2], 0, -1), send(held[2:], 0, 1)
    [other_next] = products(d_gu, (group(1, 1) + group(1, 3), BF16))
    arrived = core(other_next)
    [dx] = call(
        part(dx_kernel, n),
        [jax.ShapeDtypeStruct((1, tok, width), BF16)],
        [VMEM((blocks, tok, B), F32), VMEM((tok, width), BF16), sems((4,))],
        [tab],
        [d_gu, w],
        8,
        4 * n * product,
        out_space=pltpu.HBM,
    )
    low, high, dx, d_gu = together(low, high, dx, d_gu)
    both = (own_next + arrived.astype(F32)).reshape(2, SIDE, B, 3 * B)
    to_back = jnp.concatenate([plus(both[0, :2], low), both[0, 2:].astype(BF16)], axis=0)
    to_ahead = jnp.concatenate([both[1, :2].astype(BF16), plus(both[1, 2:], high)], axis=0)
    to_back, to_ahead, x_late, d_gu = together(to_back, to_ahead, x_late, d_gu)
    from_ahead, from_back = send(to_back, 0, -1), send(to_ahead, 0, 1)
    other_last, own_last = products(d_gu, (group(1, 0), BF16), (group(0, 0), F32))
    last = core(other_last)
    [h_next] = call(
        part(forward_next_kernel, n),
        [kept((n + 1, tok, B), BF16)],
        [VMEM((n, tok, 2 * B), F32)],
        [tab],
        [x_late, w],
        6,
        4 * n * product,
    )
    from_ahead, from_back, h_next = together(from_ahead, from_back, h_next)
    row = own_last + last.astype(F32) + from_ahead.astype(F32) + from_back.astype(F32)
    row, h_next = together(row, h_next)
    [y] = call(
        part(down_next_kernel, n),
        [jax.ShapeDtypeStruct((1, tok, width), BF16)],
        [VMEM((blocks, tok, B), F32), VMEM((tok, width), BF16), sems((4,))],
        [tab],
        [h_next, w],
        8,
        4 * n * product,
        out_space=pltpu.HBM,
    )
    out = row[1:].astype(BF16)
    one, two, three = send(out[0], -1, 0), send(out[1], 2, 0), send(out[2], 1, 0)
    one, two, three, y = together(one, two, three, y)
    grad_gu, grad_down = call(
        total_kernel,
        [
            jax.ShapeDtypeStruct((1, 1, 1, 2, B, B), F32),
            jax.ShapeDtypeStruct((1, 1, 1, B, B), F32),
        ],
        [],
        [],
        [row[0], one, two, three],
        2,
        product,
    )
    return (y, dx, grad_gu, grad_down)


def solution(mesh):
    placed = (
        P("pipe", "tile", None),
        P("pipe", "tile", None),
        P("pipe", "tile", None),
        P("pipe", None, None),
        P("pipe", None, None),
        P("pipe", None),
        P("pipe", None, None),
        P("pipe", None, None),
        P("pipe", None),
        P("pipe", "tile", None, None, None, None),
        P("pipe", "tile", None, None, None),
    )
    return jax.shard_map(
        per_device,
        mesh=mesh,
        in_specs=placed,
        out_specs=(
            P("pipe", "tile", None),
            P("pipe", "tile", None),
            P("pipe", "tile", None, None, None, None),
            P("pipe", "tile", None, None, None),
        ),
        check_vma=False,
    )
```

```python
import functools

import jax
import jax.numpy as jnp
import numpy as np
from jax import lax
from jax.experimental import pallas as pl
from jax.experimental.pallas import tpu as pltpu
from jax.sharding import PartitionSpec as P

B = 128
SIDE = 4
CHIPS = SIDE * SIDE
F32 = jnp.float32
BF16 = jnp.bfloat16
UNROLL = 16
ROWS, LEAD, FIRST, HSLOT, DCOLS, OWNER, GLIVE, DLIVE = range(8)

OTHER = (0, 0, 0, 1, 0, 1, 1, 1)
STEPS = (0, 1, 3, 0, 2, 1, 3, 2)


def group(other, j):
    [g] = [g for g in range(len(STEPS)) if (OTHER[g], STEPS[g]) == (other, j)]
    return [g * SIDE + i for i in range(SIDE)]


def pairs(first, second, core=0):
    out = []
    for x in range(SIDE):
        for y in range(SIDE):
            for c in range(2):
                dx, dy = (second, first) if c else (first, second)
                to = ((x + dx) % SIDE) * SIDE + (y + dy) % SIDE
                out.append(((x * SIDE + y) * 2 + c, to * 2 + (c + core) % 2))
    return out


def send(value, first, second, core=0):
    return lax.ppermute(value, "tile", pairs(first, second, core))


def together(*values):
    return lax.optimization_barrier(values)


def core(value):
    return send(value, 0, 0, 1)


def plus(a, b):
    return (a.astype(F32) + b.astype(F32)).astype(BF16)


def loop(count, unroll, body):
    def group(i, carry):
        body([i * unroll + u for u in range(unroll)])
        return carry

    lax.fori_loop(0, count // unroll, group, 0)


def cols(block_index):
    return pl.ds(pl.multiple_of(block_index * B, B), B)


def live(tab, row, slot):
    return tab[row, slot].astype(F32)


def rounded(value):
    return value.astype(BF16).astype(F32)


def dot(a, b, contract_a=1, contract_b=0):
    return lax.dot_general(
        a, b, (((contract_a,), (contract_b,)), ((), ())), preferred_element_type=F32
    )


SMEM, VMEM = pltpu.SMEM, pltpu.VMEM


def kept(shape, dtype):
    return pltpu.VMEM(shape, dtype)


def call(body, outs, scratch, scalars, arrays, limit, flops=0, far=(), out_space=VMEM, aliases={}):
    return pl.pallas_call(
        body,
        out_shape=outs,
        in_specs=[pl.BlockSpec(memory_space=SMEM) for _ in scalars]
        + [pl.BlockSpec(memory_space=pltpu.HBM) for _ in far]
        + [pl.BlockSpec(memory_space=VMEM) for _ in arrays],
        out_specs=[pl.BlockSpec(memory_space=out_space) for _ in outs],
        scratch_shapes=scratch,
        input_output_aliases=aliases,
        compiler_params=pltpu.CompilerParams(vmem_limit_bytes=limit << 20),
        cost_estimate=pl.CostEstimate(flops=flops, bytes_accessed=flops // 256, transcendentals=0),
    )(*scalars, *[pltpu.with_memory_space_constraint(a, pltpu.HBM) for a in far], *[pltpu.with_memory_space_constraint(a, VMEM) for a in arrays])


def row_copies(source, out, sems):
    count = sems.shape[0]
    each = out.shape[0] // count
    rows = [pl.ds(q * each, each) for q in range(count)]
    return [pltpu.make_async_copy(source.at[0, r], out.at[r], sems.at[q]) for q, r in enumerate(rows)]


def pack_kernel(gate_up, down, pending, out, held, sems, row_sems):
    copies = [
        pltpu.make_async_copy(gate_up.at[0, 0, 0], out.at[pl.ds(0, 2)], sems.at[0]),
        pltpu.make_async_copy(down.at[0, 0, 0], out.at[2], sems.at[1]),
        *row_copies(pending, held, row_sems),
    ]
    for copy in copies:
        copy.start()
    for copy in copies:
        copy.wait()


def pick_kernel(n, asked, pending, out):
    for k in range(n):
        out[k] = pending[:, cols(asked[0, k])]


def saved_kernel(n, tab, x_saved, x_next, out, turned, later, x, sems, later_sems):
    now, then = row_copies(x_saved, x, sems), row_copies(x_next, later, later_sems)
    for copy in now + then:
        copy.start()
    for copy in now:
        copy.wait()
    for k in range(n):
        block = x[:, cols(tab[ROWS, k])]
        out[k] = block
        turned[k] = block.T
    for copy in then:
        copy.wait()


def project(tab, slots, x_of, w_of, acc):
    parts = [rounded(dot(x_of(k), w_of(k)) * live(tab, GLIVE, k)) for k in slots]
    for k, part in zip(slots, parts):
        lead = tab[LEAD, k]
        acc[lead] = jnp.where(tab[FIRST, k] == 1, part, acc[lead] + part)


def project_pieces(tab, start, x, pieces, w, acc):
    places = [(piece, i) for piece in pieces for i in range(piece.shape[0])]

    def w_of(k):
        piece, i = places[k - start]
        gate, up = piece[i, 0], piece[i, 1]
        w[k, :, :B], w[k, :, B : 2 * B], w[k, :, 2 * B :] = gate, up, piece[i, 2]
        return jnp.concatenate([gate, up], axis=1)

    project(tab, range(start, start + len(places)), lambda k: x[k], w_of, acc)


def saved_first_kernel(tab, x, *refs):
    *pieces, w, acc = refs
    project_pieces(tab, 0, x, pieces, w, acc)


def saved_more_kernel(start, tab, x, *refs):
    *pieces, _, _, w, acc = refs
    project_pieces(tab, start, x, pieces, w, acc)


def saved_last_kernel(n, start, tab, x, *refs):
    *pieces, _, _, w, acc, coef, h_turned = refs
    project_pieces(tab, start, x, pieces, w, acc)

    def activate(ks):
        for k in ks:
            gate, up = acc[k, :, :B], acc[k, :, B:]
            sig = jax.nn.sigmoid(gate)
            act = gate * sig
            h_turned[k] = (act * up).astype(BF16).T
            coef[k, :, :B] = up * sig * (1.0 + gate * (1.0 - sig))
            coef[k, :, B:] = act

    loop(n, 4, activate)
    h_turned[n] = jnp.zeros((B, B), BF16)


def put(acc, out, staged, sems):
    chunks = sems.shape[0]
    each = acc.shape[0] // chunks
    copies = []
    for q in range(chunks):
        for c in range(q * each, (q + 1) * each):
            staged[:, c * B : (c + 1) * B] = acc[c].astype(BF16)
        span = pl.ds(q * each * B, each * B)
        copy = pltpu.make_async_copy(staged.at[:, span], out.at[0, :, span], sems.at[q])
        copy.start()
        copies.append(copy)
    for copy in copies:
        copy.wait()


def forward_next_kernel(n, tab, x, w, h, acc):
    def some(ks):
        project(tab, ks, lambda k: x[:, cols(tab[ROWS, k])], lambda k: w[k, :, : 2 * B], acc)

    loop(n, UNROLL, some)

    def activate(ks):
        for k in ks:
            gate, up = acc[k, :, :B], acc[k, :, B:]
            h[k] = (gate * jax.nn.sigmoid(gate) * up).astype(BF16)

    loop(n, 4, activate)
    h[n] = jnp.zeros((B, B), BF16)


def down_next_kernel(n, tab, h, w, y, acc, staged, sems):
    acc[...] = jnp.zeros_like(acc)

    def down(js):
        parts = [rounded(dot(h[tab[HSLOT, j]], w[j, :, 2 * B :]) * live(tab, DLIVE, j)) for j in js]
        for j, part in zip(js, parts):
            acc[tab[DCOLS, j]] += part

    loop(n, UNROLL, down)
    put(acc, y, staged, sems)


def grads(tab, slots, x_turned, h_turned, d_gu, cot, out):
    for k, s in enumerate(slots):
        gu = dot(x_turned[s], d_gu[tab[LEAD, s]]) * live(tab, GLIVE, s)
        down = dot(h_turned[tab[HSLOT, s]], cot[tab[OWNER, s]]) * live(tab, DLIVE, s)
        out[k, :, : 2 * B] = gu.astype(out.dtype)
        out[k, :, 2 * B :] = down.astype(out.dtype)


def backward_kernel(n, slots, tab, x_turned, w, coef, h_turned, cot, others, d_gu, dh):
    dh[...] = jnp.zeros_like(dh)

    def down(js):
        parts = [dot(cot[tab[OWNER, j]], w[j, :, 2 * B :], 1, 1) * live(tab, DLIVE, j) for j in js]
        for j, part in zip(js, parts):
            dh[tab[HSLOT, j]] += rounded(part)

    loop(n, UNROLL, down)

    def scale(ks):
        for k in ks:
            d_gu[k, :, :B] = (dh[k] * coef[k, :, :B]).astype(BF16)
            d_gu[k, :, B:] = (dh[k] * coef[k, :, B:]).astype(BF16)

    loop(n, 4, scale)
    grads(tab, slots, x_turned, h_turned, d_gu, cot, others)


def grads_kernel(slots, tab, x_turned, h_turned, d_gu, cot, *outs):
    for some, out in zip(slots, outs):
        grads(tab, some, x_turned, h_turned, d_gu, cot, out)


def dx_kernel(n, tab, d_gu, w, dx, acc, staged, sems):
    acc[...] = jnp.zeros_like(acc)

    def back(ks):
        parts = [
            rounded(dot(d_gu[tab[LEAD, k]], w[k, :, : 2 * B], 1, 1) * live(tab, GLIVE, k)) for k in ks
        ]
        for k, part in zip(ks, parts):
            acc[tab[ROWS, k]] += part

    loop(n, UNROLL, back)
    put(acc, dx, staged, sems)


def second_kernel(own, other, low, high, back, ahead):
    half = low.shape[0]
    for i in range(SIDE):
        to_back = own[i] + other[i].astype(F32)
        to_ahead = own[SIDE + i] + other[SIDE + i].astype(F32)
        if i < half:
            to_back += low[i].astype(F32)
        else:
            to_ahead += high[i - half].astype(F32)
        back[i] = to_back.astype(BF16)
        ahead[i] = to_ahead.astype(BF16)


def total_kernel(row, one, two, three, grad_gu, grad_down):
    total = row[...] + (one[...].astype(F32) + two[...].astype(F32) + three[...].astype(F32))
    grad_gu[0, 0, 0, 0] = total[:, :B]
    grad_gu[0, 0, 0, 1] = total[:, B : 2 * B]
    grad_down[0, 0, 0] = total[:, 2 * B :]


def tables(mine, g_rows, g_cols, g_live, d_rows, d_cols, d_live):
    n = g_rows.shape[0]
    ids = jnp.arange(n, dtype=jnp.int32)
    kind = (np.repeat(np.array(OTHER, np.int32), SIDE) + mine) % 2
    j, i = np.repeat(np.array(STEPS, np.int32), SIDE), ids % SIDE
    x = (mine // (2 * SIDE) - jnp.where(kind == 0, i, j)) % SIDE
    y = ((mine // 2) % SIDE - jnp.where(kind == 0, j, i)) % SIDE
    owner = (x * SIDE + y) * 2 + kind
    chosen = owner[:, None] == ids[None, :]

    def by_slot(values):
        return jnp.sum(jnp.where(chosen, values[None, :], 0), axis=1)

    rows, columns = by_slot(g_rows), by_slot(g_cols)
    lead = jnp.min(jnp.where(columns[:, None] == columns[None, :], ids[None, :], n), axis=1)
    first = (lead == ids).astype(jnp.int32)
    hslot = jnp.min(jnp.where(by_slot(d_rows)[:, None] == columns[None, :], ids[None, :], n), axis=1)
    g_on, d_on = ((by_slot(v) > 0).astype(jnp.int32) for v in (g_live, d_live))
    return jnp.stack([rows, lead, first, hslot, by_slot(d_cols), owner, g_on, d_on])


def per_device(
    x_next,
    x_saved,
    pending,
    gu_rows,
    gu_cols,
    gu_live,
    down_rows,
    down_cols,
    down_live,
    gate_up_tiles,
    down_tiles,
):
    n = lax.axis_size("tile")
    sections = lax.axis_size("pipe")
    mine = lax.axis_index("tile").astype(jnp.int32)
    tok, width = x_next.shape[1:]
    blocks = width // B
    part = functools.partial
    product = 2 * tok * B * B

    up_pairs = [(s, (s + 1) % sections) for s in range(sections)]
    down_pairs = [(s, (s - 1) % sections) for s in range(sections)]
    asked = lax.ppermute(down_cols[0].reshape(1, n), "pipe", up_pairs)
    rows, sems = kept((tok, width), BF16), pltpu.SemaphoreType.DMA
    own, held_back = call(
        pack_kernel,
        [kept((3, B, B), BF16), rows],
        [sems((2,)), sems((8,))],
        [],
        [],
        2,
        far=[gate_up_tiles, down_tiles, pending],
    )
    own, asked = together(own[None], asked)
    one, three, two = send(own, 1, 0), send(own, -1, 0), send(own, 2, 0)
    [picked] = call(
        part(pick_kernel, n), [kept((n, tok, B), BF16)], [], [asked], [held_back], 2
    )
    cot = lax.ppermute(picked, "pipe", down_pairs)
    near = jnp.concatenate([own, one, two, three], axis=0)
    near, gu_rows, gu_cols, down_rows = together(near, gu_rows, gu_cols, down_rows)
    back, ahead = send(near, 0, 1), send(near, 0, -1)

    tab = tables(
        mine,
        gu_rows[0].reshape(-1),
        gu_cols[0].reshape(-1),
        gu_live[0],
        down_rows[0].reshape(-1),
        down_cols[0].reshape(-1),
        down_live[0],
    )
    x_blocks, x_turned, x_late = call(
        part(saved_kernel, n),
        [kept((n, tok, B), BF16), kept((n, B, tok), BF16), rows],
        [VMEM((tok, width), BF16), sems((8,)), sems((8,))],
        [tab],
        [],
        4,
        far=[x_saved, x_next],
    )
    near, x_blocks, x_turned = together(near, x_blocks, x_turned)
    near_core = core(near)
    back, ahead, near_core, x_blocks, x_turned = together(back, ahead, near_core, x_blocks, x_turned)
    low, high = send(back[:2], 0, 1), send(ahead[2:], 0, -1)
    tiles, gates = kept((n, B, 3 * B), BF16), kept((n, tok, 2 * B), F32)
    w, acc = call(
        saved_first_kernel, [tiles, gates], [], [tab], [x_blocks, near, back, ahead, near_core], 6
    )
    low, high, w, acc = together(low, high, w, acc)
    more = [low, high, core(back), core(ahead)]
    w, acc = call(
        part(saved_more_kernel, CHIPS),
        [tiles, gates],
        [],
        [tab],
        [x_blocks, *more, w, acc],
        6,
        aliases={6: 0, 7: 1},
    )
    last = [core(low), core(high)]
    w, acc, coef, h_turned = call(
        part(saved_last_kernel, n, n - SIDE),
        [tiles, gates, gates, kept((n + 1, B, tok), BF16)],
        [],
        [tab],
        [x_blocks, *last, w, acc],
        6,
        aliases={4: 0, 5: 1},
    )
    other_first, d_gu = call(
        part(backward_kernel, n, group(1, 2)),
        [kept((SIDE, B, 3 * B), BF16), kept((n, tok, 2 * B), BF16)],
        [VMEM((n + 1, tok, B), F32)],
        [tab],
        [x_turned, w, coef, h_turned, cot],
        6,
    )

    def products(d_gu, *outs):
        return call(
            part(grads_kernel, [slots for slots, _ in outs]),
            [kept((len(slots), B, 3 * B), dtype) for slots, dtype in outs],
            [],
            [tab],
            [x_turned, h_turned, d_gu, cot],
            4,
        )

    first = core(other_first)
    own_first, own_next = products(d_gu, (group(0, 2), F32), (group(0, 1) + group(0, 3), F32))
    held = plus(own_first, first)
    held, own_next, d_gu = together(held, own_next, d_gu)
    low, high = send(held[:2], 0, -1), send(held[2:], 0, 1)
    [other_next] = products(d_gu, (group(1, 1) + group(1, 3), BF16))
    arrived = core(other_next)
    [dx] = call(
        part(dx_kernel, n),
        [jax.ShapeDtypeStruct((1, tok, width), BF16)],
        [VMEM((blocks, tok, B), F32), VMEM((tok, width), BF16), sems((4,))],
        [tab],
        [d_gu, w],
        8,
        4 * n * product,
        out_space=pltpu.HBM,
    )
    low, high, dx, d_gu = together(low, high, dx, d_gu)
    to_back, to_ahead = call(
        second_kernel,
        [kept((SIDE, B, 3 * B), BF16), kept((SIDE, B, 3 * B), BF16)],
        [],
        [],
        [own_next, arrived, low, high],
        2,
    )
    to_back, to_ahead, x_late, d_gu = together(to_back, to_ahead, x_late, d_gu)
    from_ahead, from_back = send(to_back, 0, -1), send(to_ahead, 0, 1)
    other_last, own_last = products(d_gu, (group(1, 0), BF16), (group(0, 0), F32))
    last = core(other_last)
    [h_next] = call(
        part(forward_next_kernel, n),
        [kept((n + 1, tok, B), BF16)],
        [VMEM((n, tok, 2 * B), F32)],
        [tab],
        [x_late, w],
        6,
        4 * n * product,
    )
    from_ahead, from_back, h_next = together(from_ahead, from_back, h_next)
    row = own_last + last.astype(F32) + from_ahead.astype(F32) + from_back.astype(F32)
    row, h_next = together(row, h_next)
    [y] = call(
        part(down_next_kernel, n),
        [jax.ShapeDtypeStruct((1, tok, width), BF16)],
        [VMEM((blocks, tok, B), F32), VMEM((tok, width), BF16), sems((4,))],
        [tab],
        [h_next, w],
        8,
        4 * n * product,
        out_space=pltpu.HBM,
    )
    out = row[1:].astype(BF16)
    one, two, three = send(out[0], -1, 0), send(out[1], 2, 0), send(out[2], 1, 0)
    one, two, three, y = together(one, two, three, y)
    grad_gu, grad_down = call(
        total_kernel,
        [
            jax.ShapeDtypeStruct((1, 1, 1, 2, B, B), F32),
            jax.ShapeDtypeStruct((1, 1, 1, B, B), F32),
        ],
        [],
        [],
        [row[0], one, two, three],
        2,
        product,
    )
    return (y, dx, grad_gu, grad_down)


def solution(mesh):
    placed = (
        P("pipe", "tile", None),
        P("pipe", "tile", None),
        P("pipe", "tile", None),
        P("pipe", None, None),
        P("pipe", None, None),
        P("pipe", None),
        P("pipe", None, None),
        P("pipe", None, None),
        P("pipe", None),
        P("pipe", "tile", None, None, None, None),
        P("pipe", "tile", None, None, None),
    )
    return jax.shard_map(
        per_device,
        mesh=mesh,
        in_specs=placed,
        out_specs=(
            P("pipe", "tile", None),
            P("pipe", "tile", None),
            P("pipe", "tile", None, None, None, None),
            P("pipe", "tile", None, None, None),
        ),
        check_vma=False,
    )
```

```python
import functools

import jax
import jax.numpy as jnp
import numpy as np
from jax import lax
from jax.experimental import pallas as pl
from jax.experimental.pallas import tpu as pltpu
from jax.sharding import PartitionSpec as P

B = 128
SIDE = 4
CHIPS = SIDE * SIDE
F32 = jnp.float32
BF16 = jnp.bfloat16
UNROLL = 16
ROWS, LEAD, FIRST, HSLOT, DCOLS, OWNER, GLIVE, DLIVE = range(8)

OTHER = (0, 0, 0, 1, 0, 1, 1, 1)
STEPS = (0, 1, 3, 0, 2, 1, 3, 2)


def group(other, j):
    [g] = [g for g in range(len(STEPS)) if (OTHER[g], STEPS[g]) == (other, j)]
    return [g * SIDE + i for i in range(SIDE)]


def pairs(first, second, core=0):
    out = []
    for x in range(SIDE):
        for y in range(SIDE):
            for c in range(2):
                dx, dy = (second, first) if c else (first, second)
                to = ((x + dx) % SIDE) * SIDE + (y + dy) % SIDE
                out.append(((x * SIDE + y) * 2 + c, to * 2 + (c + core) % 2))
    return out


def send(value, first, second, core=0):
    return lax.ppermute(value, "tile", pairs(first, second, core))


def together(*values):
    return lax.optimization_barrier(values)


def core(value):
    return send(value, 0, 0, 1)


def plus(a, b):
    return (a.astype(F32) + b.astype(F32)).astype(BF16)


def loop(count, unroll, body):
    def group(i, carry):
        body([i * unroll + u for u in range(unroll)])
        return carry

    lax.fori_loop(0, count // unroll, group, 0)


def cols(block_index):
    return pl.ds(pl.multiple_of(block_index * B, B), B)


def live(tab, row, slot):
    return tab[row, slot].astype(F32)


def rounded(value):
    return value.astype(BF16).astype(F32)


def dot(a, b, contract_a=1, contract_b=0):
    return lax.dot_general(
        a, b, (((contract_a,), (contract_b,)), ((), ())), preferred_element_type=F32
    )


SMEM, VMEM = pltpu.SMEM, pltpu.VMEM


def kept(shape, dtype):
    return pltpu.VMEM(shape, dtype)


def call(body, outs, scratch, scalars, arrays, limit, flops=0, far=(), out_space=VMEM, aliases={}):
    return pl.pallas_call(
        body,
        out_shape=outs,
        in_specs=[pl.BlockSpec(memory_space=SMEM) for _ in scalars]
        + [pl.BlockSpec(memory_space=pltpu.HBM) for _ in far]
        + [pl.BlockSpec(memory_space=VMEM) for _ in arrays],
        out_specs=[pl.BlockSpec(memory_space=out_space) for _ in outs],
        scratch_shapes=scratch,
        input_output_aliases=aliases,
        compiler_params=pltpu.CompilerParams(vmem_limit_bytes=limit << 20),
        cost_estimate=pl.CostEstimate(flops=flops, bytes_accessed=flops // 256, transcendentals=0),
    )(*scalars, *[pltpu.with_memory_space_constraint(a, pltpu.HBM) for a in far], *[pltpu.with_memory_space_constraint(a, VMEM) for a in arrays])


def row_copies(source, out, sems):
    count = sems.shape[0]
    each = out.shape[0] // count
    rows = [pl.ds(q * each, each) for q in range(count)]
    return [pltpu.make_async_copy(source.at[0, r], out.at[r], sems.at[q]) for q, r in enumerate(rows)]


def pack_kernel(gate_up, down, out, sems):
    copies = [
        pltpu.make_async_copy(gate_up.at[0, 0, 0], out.at[pl.ds(0, 2)], sems.at[0]),
        pltpu.make_async_copy(down.at[0, 0, 0], out.at[2], sems.at[1]),
    ]
    for copy in copies:
        copy.start()
    for copy in copies:
        copy.wait()


def fetch_kernel(source, out, sems):
    copies = row_copies(source, out, sems)
    for copy in copies:
        copy.start()
    for copy in copies:
        copy.wait()


def pick_kernel(n, asked, pending, out):
    for k in range(n):
        out[k] = pending[:, cols(asked[0, k])]


def saved_kernel(n, tab, x_saved, x_next, out, turned, later, x, sems, later_sems):
    now, then = row_copies(x_saved, x, sems), row_copies(x_next, later, later_sems)
    for copy in now + then:
        copy.start()
    for copy in now:
        copy.wait()
    for k in range(n):
        block = x[:, cols(tab[ROWS, k])]
        out[k] = block
        turned[k] = block.T
    for copy in then:
        copy.wait()


def project(tab, slots, x_of, w_of, acc):
    parts = [rounded(dot(x_of(k), w_of(k)) * live(tab, GLIVE, k)) for k in slots]
    for k, part in zip(slots, parts):
        lead = tab[LEAD, k]
        acc[lead] = jnp.where(tab[FIRST, k] == 1, part, acc[lead] + part)


def project_pieces(tab, start, x, pieces, w, acc):
    places = [(piece, i) for piece in pieces for i in range(piece.shape[0])]

    def w_of(k):
        piece, i = places[k - start]
        gate, up = piece[i, 0], piece[i, 1]
        w[k, :, :B], w[k, :, B : 2 * B], w[k, :, 2 * B :] = gate, up, piece[i, 2]
        return jnp.concatenate([gate, up], axis=1)

    project(tab, range(start, start + len(places)), lambda k: x[k], w_of, acc)


def saved_first_kernel(tab, x, *refs):
    *pieces, w, acc = refs
    project_pieces(tab, 0, x, pieces, w, acc)


def saved_more_kernel(start, tab, x, *refs):
    *pieces, _, _, w, acc = refs
    project_pieces(tab, start, x, pieces, w, acc)


def saved_last_kernel(n, start, tab, x, *refs):
    *pieces, _, _, w, acc, coef, h_turned = refs
    project_pieces(tab, start, x, pieces, w, acc)

    def activate(ks):
        for k in ks:
            gate, up = acc[k, :, :B], acc[k, :, B:]
            sig = jax.nn.sigmoid(gate)
            act = gate * sig
            h_turned[k] = (act * up).astype(BF16).T
            coef[k, :, :B] = up * sig * (1.0 + gate * (1.0 - sig))
            coef[k, :, B:] = act

    loop(n, 4, activate)
    h_turned[n] = jnp.zeros((B, B), BF16)


def put(acc, out, staged, sems):
    chunks = sems.shape[0]
    each = acc.shape[0] // chunks
    copies = []
    for q in range(chunks):
        for c in range(q * each, (q + 1) * each):
            staged[:, c * B : (c + 1) * B] = acc[c].astype(BF16)
        span = pl.ds(q * each * B, each * B)
        copy = pltpu.make_async_copy(staged.at[:, span], out.at[0, :, span], sems.at[q])
        copy.start()
        copies.append(copy)
    for copy in copies:
        copy.wait()


def forward_next_kernel(n, tab, x, w, h, acc):
    def some(ks):
        project(tab, ks, lambda k: x[:, cols(tab[ROWS, k])], lambda k: w[k, :, : 2 * B], acc)

    loop(n, UNROLL, some)

    def activate(ks):
        for k in ks:
            gate, up = acc[k, :, :B], acc[k, :, B:]
            h[k] = (gate * jax.nn.sigmoid(gate) * up).astype(BF16)

    loop(n, 4, activate)
    h[n] = jnp.zeros((B, B), BF16)


def down_next_kernel(n, tab, h, w, y, acc, staged, sems):
    acc[...] = jnp.zeros_like(acc)

    def down(js):
        parts = [rounded(dot(h[tab[HSLOT, j]], w[j, :, 2 * B :]) * live(tab, DLIVE, j)) for j in js]
        for j, part in zip(js, parts):
            acc[tab[DCOLS, j]] += part

    loop(n, UNROLL, down)
    put(acc, y, staged, sems)


def grads(tab, slots, x_turned, h_turned, d_gu, cot, out):
    for k, s in enumerate(slots):
        gu = dot(x_turned[s], d_gu[tab[LEAD, s]]) * live(tab, GLIVE, s)
        down = dot(h_turned[tab[HSLOT, s]], cot[tab[OWNER, s]]) * live(tab, DLIVE, s)
        out[k, :, : 2 * B] = gu.astype(out.dtype)
        out[k, :, 2 * B :] = down.astype(out.dtype)


def backward_kernel(n, slots, tab, x_turned, w, coef, h_turned, cot, others, d_gu, dh):
    dh[...] = jnp.zeros_like(dh)

    def down(js):
        parts = [dot(cot[tab[OWNER, j]], w[j, :, 2 * B :], 1, 1) * live(tab, DLIVE, j) for j in js]
        for j, part in zip(js, parts):
            dh[tab[HSLOT, j]] += rounded(part)

    loop(n, UNROLL, down)

    def scale(ks):
        for k in ks:
            d_gu[k, :, :B] = (dh[k] * coef[k, :, :B]).astype(BF16)
            d_gu[k, :, B:] = (dh[k] * coef[k, :, B:]).astype(BF16)

    loop(n, 4, scale)
    grads(tab, slots, x_turned, h_turned, d_gu, cot, others)


def grads_kernel(slots, tab, x_turned, h_turned, d_gu, cot, *outs):
    for some, out in zip(slots, outs):
        grads(tab, some, x_turned, h_turned, d_gu, cot, out)


def dx_kernel(n, tab, d_gu, w, dx, acc, staged, sems):
    acc[...] = jnp.zeros_like(acc)

    def back(ks):
        parts = [
            rounded(dot(d_gu[tab[LEAD, k]], w[k, :, : 2 * B], 1, 1) * live(tab, GLIVE, k)) for k in ks
        ]
        for k, part in zip(ks, parts):
            acc[tab[ROWS, k]] += part

    loop(n, UNROLL, back)
    put(acc, dx, staged, sems)


def second_kernel(own, other, low, high, back, ahead):
    half = low.shape[0]
    for i in range(SIDE):
        to_back = own[i] + other[i].astype(F32)
        to_ahead = own[SIDE + i] + other[SIDE + i].astype(F32)
        if i < half:
            to_back += low[i].astype(F32)
        else:
            to_ahead += high[i - half].astype(F32)
        back[i] = to_back.astype(BF16)
        ahead[i] = to_ahead.astype(BF16)


def total_kernel(row, one, two, three, grad_gu, grad_down):
    total = row[...] + (one[...].astype(F32) + two[...].astype(F32) + three[...].astype(F32))
    grad_gu[0, 0, 0, 0] = total[:, :B]
    grad_gu[0, 0, 0, 1] = total[:, B : 2 * B]
    grad_down[0, 0, 0] = total[:, 2 * B :]


def tables(mine, g_rows, g_cols, g_live, d_rows, d_cols, d_live):
    n = g_rows.shape[0]
    ids = jnp.arange(n, dtype=jnp.int32)
    kind = (np.repeat(np.array(OTHER, np.int32), SIDE) + mine) % 2
    j, i = np.repeat(np.array(STEPS, np.int32), SIDE), ids % SIDE
    x = (mine // (2 * SIDE) - jnp.where(kind == 0, i, j)) % SIDE
    y = ((mine // 2) % SIDE - jnp.where(kind == 0, j, i)) % SIDE
    owner = (x * SIDE + y) * 2 + kind
    chosen = owner[:, None] == ids[None, :]

    def by_slot(values):
        return jnp.sum(jnp.where(chosen, values[None, :], 0), axis=1)

    rows, columns = by_slot(g_rows), by_slot(g_cols)
    lead = jnp.min(jnp.where(columns[:, None] == columns[None, :], ids[None, :], n), axis=1)
    first = (lead == ids).astype(jnp.int32)
    hslot = jnp.min(jnp.where(by_slot(d_rows)[:, None] == columns[None, :], ids[None, :], n), axis=1)
    g_on, d_on = ((by_slot(v) > 0).astype(jnp.int32) for v in (g_live, d_live))
    return jnp.stack([rows, lead, first, hslot, by_slot(d_cols), owner, g_on, d_on])


def per_device(
    x_next,
    x_saved,
    pending,
    gu_rows,
    gu_cols,
    gu_live,
    down_rows,
    down_cols,
    down_live,
    gate_up_tiles,
    down_tiles,
):
    n = lax.axis_size("tile")
    sections = lax.axis_size("pipe")
    mine = lax.axis_index("tile").astype(jnp.int32)
    tok, width = x_next.shape[1:]
    blocks = width // B
    part = functools.partial
    product = 2 * tok * B * B

    up_pairs = [(s, (s + 1) % sections) for s in range(sections)]
    down_pairs = [(s, (s - 1) % sections) for s in range(sections)]
    asked = lax.ppermute(down_cols[0].reshape(1, n), "pipe", up_pairs)
    rows, sems = kept((tok, width), BF16), pltpu.SemaphoreType.DMA
    [own] = call(
        pack_kernel,
        [kept((3, B, B), BF16)],
        [sems((2,))],
        [],
        [],
        2,
        far=[gate_up_tiles, down_tiles],
    )
    own = own[None]
    one, three, two = send(own, 1, 0), send(own, -1, 0), send(own, 2, 0)
    [held_back] = call(fetch_kernel, [rows], [sems((8,))], [], [], 2, far=[pending])
    [picked] = call(
        part(pick_kernel, n), [kept((n, tok, B), BF16)], [], [asked], [held_back], 2
    )
    cot = lax.ppermute(picked, "pipe", down_pairs)
    near = jnp.concatenate([own, one, two, three], axis=0)
    near, gu_rows, gu_cols, down_rows = together(near, gu_rows, gu_cols, down_rows)
    back, ahead = send(near, 0, 1), send(near, 0, -1)

    tab = tables(
        mine,
        gu_rows[0].reshape(-1),
        gu_cols[0].reshape(-1),
        gu_live[0],
        down_rows[0].reshape(-1),
        down_cols[0].reshape(-1),
        down_live[0],
    )
    x_blocks, x_turned, x_late = call(
        part(saved_kernel, n),
        [kept((n, tok, B), BF16), kept((n, B, tok), BF16), rows],
        [VMEM((tok, width), BF16), sems((8,)), sems((8,))],
        [tab],
        [],
        4,
        far=[x_saved, x_next],
    )
    near, x_blocks, x_turned = together(near, x_blocks, x_turned)
    near_core = core(near)
    back, ahead, near_core, x_blocks, x_turned = together(back, ahead, near_core, x_blocks, x_turned)
    low, high = send(back[:2], 0, 1), send(ahead[2:], 0, -1)
    tiles, gates = kept((n, B, 3 * B), BF16), kept((n, tok, 2 * B), F32)
    w, acc = call(
        saved_first_kernel, [tiles, gates], [], [tab], [x_blocks, near, back, ahead, near_core], 6
    )
    low, high, w, acc = together(low, high, w, acc)
    more = [low, high, core(back), core(ahead)]
    w, acc = call(
        part(saved_more_kernel, CHIPS),
        [tiles, gates],
        [],
        [tab],
        [x_blocks, *more, w, acc],
        6,
        aliases={6: 0, 7: 1},
    )
    last = [core(low), core(high)]
    w, acc, coef, h_turned = call(
        part(saved_last_kernel, n, n - SIDE),
        [tiles, gates, gates, kept((n + 1, B, tok), BF16)],
        [],
        [tab],
        [x_blocks, *last, w, acc],
        6,
        aliases={4: 0, 5: 1},
    )
    other_first, d_gu = call(
        part(backward_kernel, n, group(1, 2)),
        [kept((SIDE, B, 3 * B), BF16), kept((n, tok, 2 * B), BF16)],
        [VMEM((n + 1, tok, B), F32)],
        [tab],
        [x_turned, w, coef, h_turned, cot],
        6,
    )

    def products(d_gu, *outs):
        return call(
            part(grads_kernel, [slots for slots, _ in outs]),
            [kept((len(slots), B, 3 * B), dtype) for slots, dtype in outs],
            [],
            [tab],
            [x_turned, h_turned, d_gu, cot],
            4,
        )

    first = core(other_first)
    own_first, own_next = products(d_gu, (group(0, 2), F32), (group(0, 1) + group(0, 3), F32))
    held = plus(own_first, first)
    held, own_next, d_gu = together(held, own_next, d_gu)
    low, high = send(held[:2], 0, -1), send(held[2:], 0, 1)
    [other_next] = products(d_gu, (group(1, 1) + group(1, 3), BF16))
    arrived = core(other_next)
    [dx] = call(
        part(dx_kernel, n),
        [jax.ShapeDtypeStruct((1, tok, width), BF16)],
        [VMEM((blocks, tok, B), F32), VMEM((tok, width), BF16), sems((4,))],
        [tab],
        [d_gu, w],
        8,
        4 * n * product,
        out_space=pltpu.HBM,
    )
    low, high, dx, d_gu = together(low, high, dx, d_gu)
    to_back, to_ahead = call(
        second_kernel,
        [kept((SIDE, B, 3 * B), BF16), kept((SIDE, B, 3 * B), BF16)],
        [],
        [],
        [own_next, arrived, low, high],
        2,
    )
    to_back, to_ahead, x_late, d_gu = together(to_back, to_ahead, x_late, d_gu)
    from_ahead, from_back = send(to_back, 0, -1), send(to_ahead, 0, 1)
    other_last, own_last = products(d_gu, (group(1, 0), BF16), (group(0, 0), F32))
    last = core(other_last)
    [h_next] = call(
        part(forward_next_kernel, n),
        [kept((n + 1, tok, B), BF16)],
        [VMEM((n, tok, 2 * B), F32)],
        [tab],
        [x_late, w],
        6,
        4 * n * product,
    )
    from_ahead, from_back, h_next = together(from_ahead, from_back, h_next)
    row = own_last + last.astype(F32) + from_ahead.astype(F32) + from_back.astype(F32)
    row, h_next = together(row, h_next)
    [y] = call(
        part(down_next_kernel, n),
        [jax.ShapeDtypeStruct((1, tok, width), BF16)],
        [VMEM((blocks, tok, B), F32), VMEM((tok, width), BF16), sems((4,))],
        [tab],
        [h_next, w],
        8,
        4 * n * product,
        out_space=pltpu.HBM,
    )
    out = row[1:].astype(BF16)
    one, two, three = send(out[0], -1, 0), send(out[1], 2, 0), send(out[2], 1, 0)
    one, two, three, y = together(one, two, three, y)
    grad_gu, grad_down = call(
        total_kernel,
        [
            jax.ShapeDtypeStruct((1, 1, 1, 2, B, B), F32),
            jax.ShapeDtypeStruct((1, 1, 1, B, B), F32),
        ],
        [],
        [],
        [row[0], one, two, three],
        2,
        product,
    )
    return (y, dx, grad_gu, grad_down)


def solution(mesh):
    placed = (
        P("pipe", "tile", None),
        P("pipe", "tile", None),
        P("pipe", "tile", None),
        P("pipe", None, None),
        P("pipe", None, None),
        P("pipe", None),
        P("pipe", None, None),
        P("pipe", None, None),
        P("pipe", None),
        P("pipe", "tile", None, None, None, None),
        P("pipe", "tile", None, None, None),
    )
    return jax.shard_map(
        per_device,
        mesh=mesh,
        in_specs=placed,
        out_specs=(
            P("pipe", "tile", None),
            P("pipe", "tile", None),
            P("pipe", "tile", None, None, None, None),
            P("pipe", "tile", None, None, None),
        ),
        check_vma=False,
    )
```
